256 devices in a mesh: dp: 2 (over z_lo), station: 8 (over y, core), tm: 16 (over z_hi, x).
Axes of the slice: x: 4, y: 4, z: 8 (z_hi: 4, z_lo: 2; z = z_hi * 2 + z_lo), core: 2. Of those that a mesh axis runs over, the one named last changes fastest.
Arguments:
- inputs: bfloat16 [2, 256, 256, 512], P('dp', 'station', 'tm'), may hold values from -6 to 6
- cotangent: bfloat16 [2, 256, 256, 512], P('dp', 'station', 'tm'), may hold values from -6 to 6
- station_gain: float32 [512], replicated, may hold values from 0.5 to 1.5
- station_qkv: bfloat16 [512, 1536], replicated, may hold values from -0.25 to 0.25
- station_out: bfloat16 [512, 512], replicated, may hold values from -0.25 to 0.25
- time_gain: float32 [512], replicated, may hold values from 0.5 to 1.5
- time_qkv: bfloat16 [512, 1536], replicated, may hold values from -0.25 to 0.25
- time_out: bfloat16 [512, 512], replicated, may hold values from -0.25 to 0.25
Outputs:
- grad_inputs: bfloat16 [2, 256, 256, 512], P('dp', 'station', 'tm')
- grad_station_qkv: bfloat16 [512, 1536], P('station', 'tm')
- grad_station_out: bfloat16 [512, 512], P('station', 'tm')
- grad_station_gain: float32 [512], replicated
- grad_time_qkv: bfloat16 [512, 1536], P('station', 'tm')
- grad_time_out: bfloat16 [512, 512], P('station', 'tm')
- grad_time_gain: float32 [512], replicated
The draws below stay inside these ranges and needn't reach their ends.
All inputs are finite; a program needn't handle non-finite values.
Results may differ from the reference program's by a relative error of at most 0.03.
Values may be sent and summed in bfloat16 or wider, within the bound.
A program may use at most 128 MiB of HBM per device.

```python
import math
import jax
import jax.numpy as jnp
from jax import lax

D = 512
HEADS = 8
SAMPLES = 2
STATIONS = 256
EPOCHS = 256


def levels(key, extent, cuts, low, high):
    factor_of = 1.0
    for position, shards_of in cuts:
        steps = jax.random.uniform(jax.random.fold_in(jax.random.fold_in(key, 6), position), (shards_of,), jnp.float32, low / len(cuts), high / len(cuts))
        factor_of = factor_of * jnp.repeat(jnp.exp(steps), extent[position] // shards_of).reshape((-1,) + (1,) * (len(extent) - 1 - position))
    return factor_of


def normal_values(own_key, extent, spread, reach, cuts=(), kind=jnp.bfloat16):
    values = spread * jax.random.normal(own_key, extent, jnp.float32)
    if cuts:
        values = values * levels(own_key, extent, cuts, -0.22, 0.18)
    return jnp.clip(values, -reach, reach).astype(kind)


def setup_inputs(seed: int = 0) -> dict:
    splits = jax.random.split(jax.random.key(seed), 9)
    inputs = normal_values(splits[0], (SAMPLES, STATIONS, EPOCHS, D), 1.0, 6.0, ((0, 2), (1, 8), (2, 16)))
    cotangent = normal_values(splits[1], (SAMPLES, STATIONS, EPOCHS, D), 1.0, 6.0, ((0, 2), (1, 8), (2, 16)))
    station_gain = jnp.clip(1.0 + 0.1 * jax.random.normal(splits[2], (D,), jnp.float32), 0.5, 1.5)
    station_qkv = normal_values(splits[3], (D, 3 * D), D ** -0.5, 0.25)
    station_out = normal_values(splits[4], (D, D), D ** -0.5, 0.25)
    time_gain = jnp.clip(1.0 + 0.1 * jax.random.normal(splits[5], (D,), jnp.float32), 0.5, 1.5)
    time_qkv = normal_values(splits[6], (D, 3 * D), D ** -0.5, 0.25)
    time_out = normal_values(splits[7], (D, D), D ** -0.5, 0.25)
    return dict(inputs=inputs, cotangent=cotangent, station_gain=station_gain, station_qkv=station_qkv, station_out=station_out, time_gain=time_gain, time_qkv=time_qkv, time_out=time_out)


EPSILON = 1e-05

def stored(values):
    return lax.optimization_barrier(values.astype(jnp.bfloat16))

def layer_parts(inputs, gains, w_qkv):
    groups, length, inner, width = inputs.shape
    heads_dim = width // HEADS
    head_shape = (groups, length, inner, HEADS, heads_dim)
    rows_full = inputs.reshape(groups * length * inner, width).astype(jnp.float32)
    inverse = lax.rsqrt(lax.optimization_barrier(jnp.mean(rows_full * rows_full, axis=1, keepdims=True)) + EPSILON)
    normed = rows_full * inverse
    acted = stored(normed * gains)
    joined = stored(jnp.dot(acted, w_qkv, preferred_element_type=jnp.float32))
    queries = joined[:, :width].reshape(head_shape)
    keys_part = joined[:, width:2 * width].reshape(head_shape)
    values_part = joined[:, 2 * width:].reshape(head_shape)
    scale = heads_dim ** (-0.5)
    scores = jnp.einsum('alche,amche->achlm', queries.astype(jnp.float32), keys_part.astype(jnp.float32)) * scale
    expon = jnp.exp(scores)
    weights_full = expon / lax.optimization_barrier(jnp.sum(expon, axis=-1, keepdims=True))
    weights_half = stored(weights_full)
    attended = stored(jnp.einsum('achlm,amche->alche', weights_half.astype(jnp.float32), values_part.astype(jnp.float32))).reshape(-1, width)
    return (rows_full, inverse, normed, acted, queries, keys_part, values_part, weights_full, weights_half, attended)

def layer_forward(inputs, gains, w_qkv, w_out):
    parts = layer_parts(inputs, gains, w_qkv)
    return (parts[0] + jnp.dot(parts[9], w_out, preferred_element_type=jnp.float32)).astype(jnp.bfloat16).reshape(inputs.shape)

def layer_backward(inputs, upstream, gains, w_qkv, w_out):
    rows_full, inverse, normed, acted, queries, keys_part, values_part, weights_full, weights_half, attended = layer_parts(inputs, gains, w_qkv)
    width = inputs.shape[3]
    head_shape = queries.shape
    scale = head_shape[4] ** (-0.5)
    up_rows = upstream.reshape(-1, width)
    grad_out = lax.dot_general(attended, up_rows, (((0,), (0,)), ((), ())), preferred_element_type=jnp.float32)
    grad_att = stored(lax.dot_general(up_rows, w_out, (((1,), (1,)), ((), ())), preferred_element_type=jnp.float32)).reshape(head_shape)
    grad_weights = jnp.einsum('alche,amche->achlm', grad_att.astype(jnp.float32), values_part.astype(jnp.float32))
    grad_values = stored(jnp.einsum('achlm,alche->amche', weights_half.astype(jnp.float32), grad_att.astype(jnp.float32)))
    row_dot = lax.optimization_barrier(jnp.sum(grad_weights * weights_full, axis=-1, keepdims=True))
    grad_scores = stored(weights_full * (grad_weights - row_dot) * scale)
    grad_queries = stored(jnp.einsum('achlm,amche->alche', grad_scores.astype(jnp.float32), keys_part.astype(jnp.float32)))
    grad_keys = stored(jnp.einsum('achlm,alche->amche', grad_scores.astype(jnp.float32), queries.astype(jnp.float32)))
    grad_joined = jnp.concatenate([grad_queries.reshape(-1, width), grad_keys.reshape(-1, width), grad_values.reshape(-1, width)], axis=1)
    grad_qkv = lax.dot_general(acted, grad_joined, (((0,), (0,)), ((), ())), preferred_element_type=jnp.float32)
    grad_acted = lax.dot_general(grad_joined, w_qkv, (((1,), (1,)), ((), ())), preferred_element_type=jnp.float32)
    grad_gain = lax.optimization_barrier(jnp.sum(grad_acted * normed, axis=0))
    grad_normed = grad_acted * gains
    grad_rows = inverse * (grad_normed - normed * lax.optimization_barrier(jnp.mean(grad_normed * normed, axis=1, keepdims=True)))
    grad_inputs = (up_rows.astype(jnp.float32) + grad_rows).astype(jnp.bfloat16).reshape(inputs.shape)
    return (grad_inputs, grad_qkv, grad_out, grad_gain)

def blocked_forward(inputs, gains, w_qkv, w_out):
    groups = inputs.shape[0]
    block = math.gcd(groups, 8)
    pieces = inputs.reshape((groups // block, block) + inputs.shape[1:])
    outputs = lax.map(lambda piece: layer_forward(piece, gains, w_qkv, w_out), pieces)
    return outputs.reshape(inputs.shape)

def blocked_backward(inputs, upstream, gains, w_qkv, w_out):
    groups = inputs.shape[0]
    width = inputs.shape[3]
    block = math.gcd(groups, 8)
    pieces = inputs.reshape((groups // block, block) + inputs.shape[1:])
    up_pieces = upstream.reshape((groups // block, block) + inputs.shape[1:])

    def advance(carry, pair):
        grad_piece, grad_qkv, grad_out, grad_gain = layer_backward(pair[0], pair[1], gains, w_qkv, w_out)
        return ((carry[0] + grad_qkv, carry[1] + grad_out, carry[2] + grad_gain), grad_piece)
    start = (jnp.zeros((width, 3 * width), jnp.float32), jnp.zeros((width, width), jnp.float32), jnp.zeros((width,), jnp.float32))
    totals, grads = lax.scan(advance, start, (pieces, up_pieces))
    return (grads.reshape(inputs.shape), totals)

def reference(inputs, cotangent, station_gain, station_qkv, station_out, time_gain, time_qkv, time_out):
    samples, stations, epochs, width = inputs.shape
    station_view = inputs.transpose(0, 2, 1, 3).reshape(samples * epochs, stations, 1, width)
    mid_station = blocked_forward(station_view, station_gain, station_qkv, station_out)
    mid_time = mid_station.reshape(samples, epochs, stations, width).transpose(0, 2, 1, 3).reshape(samples * stations, epochs, 1, width)
    up_time = cotangent.reshape(samples * stations, epochs, 1, width)
    grad_mid, time_totals = blocked_backward(mid_time, up_time, time_gain, time_qkv, time_out)
    grad_mid_station = grad_mid.reshape(samples, stations, epochs, width).transpose(0, 2, 1, 3).reshape(samples * epochs, stations, 1, width)
    grad_station, station_totals = blocked_backward(station_view, grad_mid_station, station_gain, station_qkv, station_out)
    grad_inputs = grad_station.reshape(samples, epochs, stations, width).transpose(0, 2, 1, 3)
    return (grad_inputs, station_totals[0].astype(jnp.bfloat16), station_totals[1].astype(jnp.bfloat16), station_totals[2], time_totals[0].astype(jnp.bfloat16), time_totals[1].astype(jnp.bfloat16), time_totals[2])
```

```python
import functools

import jax
import jax.numpy as jnp
from jax import lax
from jax.experimental import pallas as pl
from jax.experimental.pallas import tpu as pltpu
from jax.sharding import PartitionSpec as P

MESH = pl.DeviceIdType.MESH
BF = jnp.bfloat16
F32 = jnp.float32
EPSILON = 1e-05
WIDTH = 512
TOKENS = 512
SEQ = 256
PAIRS = 4
PEERS = 128

R_IN, R_COT, R_MID, R_GMID, R_GIN, R_GAIN_S, R_GAIN_X, R_GAIN_Z, R_TIME, R_STATION = (
    0, 1, 2, 3, 4, 5, 6, 7, 8, 12,
)
N_SEMS = 16
L_X, L_COT, L_WQS, L_WOS, L_WQT, L_WOT = range(6)


def nn(a, b):
    return jnp.dot(a, b, preferred_element_type=F32)


def nt(a, b):
    return lax.dot_general(a, b, (((1,), (1,)), ((), ())), preferred_element_type=F32)


def columns(pair, base=0):
    return pl.ds(pl.multiple_of(base + pair * 128, 128), 128)


def half_masks(value):
    lane = lax.broadcasted_iota(jnp.int32, (1, 128), 1)
    first = jnp.where(lane < 64, value, 0.0).astype(BF)
    second = jnp.where(lane < 64, 0.0, value).astype(BF)
    return first, second


def normalise(x, gain):
    inverse = lax.rsqrt(jnp.mean(x * x, axis=1, keepdims=True) + EPSILON)
    normed = x * inverse
    return inverse, (normed * gain).astype(BF)


def softmax_t(scores):
    expon = jnp.exp(scores)
    total = jnp.sum(expon, axis=0, keepdims=True)
    shrink = jnp.where(total > 1.0, 0.25, 1.0)
    return (expon * shrink) * (1.0 / (total * shrink))


def forward_step(step, joined, probs, att_t):
    seq, pair = step // PAIRS, lax.rem(step, PAIRS)
    rows = pl.ds(pl.multiple_of(seq * SEQ, SEQ), SEQ)
    queries = joined[rows, columns(pair)]
    keys = joined[rows, columns(pair, WIDTH)]
    values_t = joined[rows, columns(pair, 2 * WIDTH)].T
    masks = half_masks(0.125)
    for head in range(2):
        p = softmax_t(nt(keys, queries * masks[head]))
        probs[2 * step + head] = p
        out = nn(values_t[64 * head : 64 * head + 64], p.astype(BF)).astype(BF)
        att_t[pl.ds(pl.multiple_of(pair * 128 + 64 * head, 64), 64), rows] = out


def backward_step(step, joined, probs, att_t, grad_att, grad_joined, grad_q_t, forward):
    seq, pair = step // PAIRS, lax.rem(step, PAIRS)
    rows = pl.ds(pl.multiple_of(seq * SEQ, SEQ), SEQ)
    queries = joined[rows, columns(pair)]
    keys = joined[rows, columns(pair, WIDTH)]
    values = joined[rows, columns(pair, 2 * WIDTH)]
    upstream = grad_att[rows, columns(pair)]
    eighths = half_masks(0.125)
    ones = half_masks(1.0)
    keys_t = (keys * jnp.asarray(0.125, BF)).T
    if forward:
        values_t = values.T
    qs, us, p_halves, grad_ss = [], [], [], []
    for head in range(2):
        half = slice(64 * head, 64 * head + 64)
        q = queries * eighths[head]
        u = upstream * ones[head]
        if forward:
            p = softmax_t(nt(keys, q))
        else:
            p = probs[2 * step + head]
        p_half = p.astype(BF)
        out_rows = pl.ds(pl.multiple_of(pair * 128 + 64 * head, 64), 64)
        if forward:
            att_t[out_rows, rows] = nn(values_t[half], p_half).astype(BF)
        grad_p = nt(values, u)
        dot = jnp.sum(grad_p * p, axis=0, keepdims=True)
        grad_s = (p * (grad_p - dot)).astype(BF)
        grad_q_t[out_rows, rows] = nn(keys_t[half], grad_s).astype(BF)
        qs.append(q)
        us.append(u)
        p_halves.append(p_half)
        grad_ss.append(grad_s)
    grad_k = nn(jnp.concatenate(grad_ss, axis=1), jnp.concatenate(qs, axis=0))
    grad_v = nn(jnp.concatenate(p_halves, axis=1), jnp.concatenate(us, axis=0))
    grad_joined[rows, columns(pair, WIDTH)] = grad_k.astype(BF)
    grad_joined[rows, columns(pair, 2 * WIDTH)] = grad_v.astype(BF)


def norm_backward(x, inverse, gain, grad_acted, upstream):
    normed = x * inverse
    grad_gain = jnp.sum(grad_acted * normed, axis=0, keepdims=True)
    grad_normed = grad_acted * gain
    mean = jnp.mean(grad_normed * normed, axis=1, keepdims=True)
    return grad_gain, upstream + inverse * (grad_normed - normed * mean)


def pack(block_of, wide, send):
    for k in range(4):
        block = block_of(k)
        for c in range(4):
            wide[pl.ds(c * 4 + k, PEERS, stride=16), :] = block[:, 128 * c : 128 * c + 128]
    send[...] = wide[...].astype(BF).reshape(PEERS, 16, 128)


def unpack(recv, wide, store):
    wide[...] = recv[...].reshape(PEERS * 16, 128).astype(F32)
    for k in range(4):
        for c in range(4):
            store(k, c, wide[pl.ds(c * 4 + k, PEERS, stride=16), :])


def kernel(
    x_hbm, cot_hbm, gain_s_ref, wq_s_hbm, wo_s_hbm, gain_t_ref, wq_t_hbm, wo_t_hbm,
    gin_ref, gq_s_ref, go_s_ref, gg_s_ref, gq_t_ref, go_t_ref, gg_t_ref,
    x_raw, fine, wide, in_send, xs, cot_recv, ups_t, wq_s, wo_s, wq_t, wo_t,
    acted, joined_s, joined_t, probs, att_t, grad_att, grad_joined, grad_q_t, acted_t,
    mid_send, mid_recv, xt, gmid_send, gmid_recv, ups_s, gin_send, gin_recv,
    total, pair_send, pair_recv, y_send, y_recv, x_send, x_recv, z_send, z_recv,
    gain_send, gain_s_recv, gain_x_recv, gain_z_recv,
    send_sems, recv_sems, local_sems,
):
    dp, station, tm = lax.axis_index("dp"), lax.axis_index("station"), lax.axis_index("tm")
    me = station * 16 + tm
    y, core = station // 2, lax.rem(station, 2)
    z_hi, x_at = tm // 4, lax.rem(tm, 4)

    def local_copy(source, target, sem):
        return pltpu.make_async_copy(source, target, local_sems.at[sem])

    def remote(source, target, sem, device):
        pltpu.make_async_remote_copy(
            src_ref=source, dst_ref=target, send_sem=send_sems.at[sem],
            recv_sem=recv_sems.at[sem], device_id=device, device_id_type=MESH,
        ).start()

    def received(ref, sem):
        pltpu.make_async_copy(ref, ref, recv_sems.at[sem]).wait()

    def sent(ref, sem):
        pltpu.make_async_copy(ref, ref, send_sems.at[sem]).wait()

    loads = [
        local_copy(x_hbm, x_raw, L_X),
        local_copy(wq_s_hbm, wq_s, L_WQS),
        local_copy(wo_s_hbm, wo_s, L_WOS),
        local_copy(cot_hbm.at[pl.ds(2 * tm, 2)], cot_recv.at[:, tm], L_COT),
        local_copy(wq_t_hbm, wq_t, L_WQT),
        local_copy(wo_t_hbm, wo_t, L_WOT),
    ]
    for load in loads:
        load.start()

    barrier = pltpu.get_barrier_semaphore()

    def greet(device):
        pl.semaphore_signal(barrier, inc=1, device_id=device, device_id_type=MESH)

    def greet_station(i, _):
        greet((dp, lax.rem(station + i, 8), tm))
        return 0

    def greet_tm(i, _):
        greet((dp, station, lax.rem(tm + i, 16)))
        return 0

    def greet_dp(i, _):
        greet((1 - dp, station, i * 4 + x_at))
        return 0

    lax.fori_loop(1, 8, greet_station, 0)
    lax.fori_loop(1, 16, greet_tm, 0)
    lax.fori_loop(0, 4, greet_dp, 0)

    loads[0].wait()
    for c in range(4):
        fine[c] = x_raw[:, :, 128 * c : 128 * c + 128].astype(F32).reshape(TOKENS, 128)
    for s in range(8):
        for e in range(2):
            for st in range(2):
                for c in range(4):
                    in_send[s, e, st, :, 128 * c : 128 * c + 128] = fine[
                        c, pl.ds(st * 16 + 2 * s + e, 16, stride=32), :
                    ].astype(BF)
    pl.semaphore_wait(barrier, 26)

    def send_in(i, _):
        p = lax.rem(station + i, 8)
        remote(in_send.at[p], xs.at[:, :, station], R_IN, (dp, p, tm))
        return 0

    lax.fori_loop(1, 8, send_in, 0)

    def send_cot(i, _):
        p = lax.rem(tm + i, 16)
        remote(cot_hbm.at[pl.ds(2 * p, 2)], cot_recv.at[:, tm], R_COT, (dp, station, p))
        return 0

    lax.fori_loop(1, 16, send_cot, 0)
    xs[:, :, station] = in_send[station]

    received(xs.at[:, :, pl.ds(0, 7)], R_IN)
    loads[1].wait()
    loads[2].wait()
    gain_s = gain_s_ref[...]
    _, acted_value = normalise(xs[...].reshape(TOKENS, WIDTH).astype(F32), gain_s)
    acted[0] = acted_value
    joined_s[...] = nn(acted_value, wq_s[...]).astype(BF)

    def forward_loop(step, _):
        forward_step(step, joined_s, probs, att_t.at[0])
        return 0

    lax.fori_loop(0, 2 * PAIRS, forward_loop, 0)
    attended = att_t[0].T
    mid = xs[...].reshape(TOKENS, WIDTH).astype(F32) + nn(attended, wo_s[...])
    pack(lambda k: mid[128 * k : 128 * k + 128], wide, mid_send)

    def send_mid(i, _):
        p = lax.rem(me + i, PEERS)
        remote(mid_send.at[p], mid_recv.at[me], R_MID, (dp, p // 16, lax.rem(p, 16)))
        return 0

    lax.fori_loop(1, PEERS, send_mid, 0)
    mid_recv[me] = mid_send[me]

    loads[3].wait()
    received(cot_recv.at[:, pl.ds(0, 15)], R_COT)
    for c in range(4):
        fine[c] = cot_recv[:, :, :, 128 * c : 128 * c + 128].astype(F32).reshape(TOKENS, 128)
    for st in range(2):
        for e in range(2):
            for s in range(8):
                row = ((st * 2 + e) * 8 + s) * 16
                for c in range(4):
                    ups_t[row : row + 16, 128 * c : 128 * c + 128] = fine[
                        c, pl.ds(st * 256 + 2 * s + e, 16, stride=16), :
                    ].astype(BF)
    loads[4].wait()
    loads[5].wait()
    grad_att[...] = nt(ups_t[...], wo_t[...]).astype(BF)
    acted_t[0] = acted[0].T

    received(mid_recv.at[pl.ds(0, PEERS - 1)], R_MID)

    def put_mid(k, c, value):
        e, st = k // 2, k % 2
        row = (st * 2 + e) * 128
        xt[row : row + 128, 128 * c : 128 * c + 128] = value

    unpack(mid_recv, wide, put_mid)
    gain_t = gain_t_ref[...]
    inverse_t, acted_value = normalise(xt[...], gain_t)
    acted[1] = acted_value
    joined_t[...] = nn(acted_value, wq_t[...]).astype(BF)
    acted_t[1] = acted_value.T

    def time_loop(step, _):
        backward_step(step, joined_t, None, att_t.at[1], grad_att, grad_joined, grad_q_t, True)
        return 0

    lax.fori_loop(0, 2 * PAIRS, time_loop, 0)
    grad_joined[:, 0:WIDTH] = grad_q_t[...].T
    grad_acted = nt(grad_joined[...], wq_t[...])
    gain_sum_t, grad_mid = norm_backward(
        xt[...], inverse_t, gain_t, grad_acted, ups_t[...].astype(F32)
    )

    def grad_mid_block(k):
        e, st = k // 2, k % 2
        row = (st * 2 + e) * 128
        return grad_mid[row : row + 128]

    pack(grad_mid_block, wide, gmid_send)

    def send_gmid(i, _):
        p = lax.rem(me + i, PEERS)
        remote(gmid_send.at[p], gmid_recv.at[me], R_GMID, (dp, p // 16, lax.rem(p, 16)))
        return 0

    lax.fori_loop(1, PEERS, send_gmid, 0)
    gmid_recv[me] = gmid_send[me]

    def sums_begin(layer, base, upstream):
        total[:, :, 0 : 3 * WIDTH] = nn(acted_t[layer], grad_joined[...]).reshape(8, 64, 3 * WIDTH)
        total[:, :, 3 * WIDTH :] = nn(att_t[layer], upstream).reshape(8, 64, WIDTH)

        def fill(i, _):
            pair_send[layer, i] = total[2 * i + 1 - core].astype(BF)
            return 0

        lax.fori_loop(0, 4, fill, 0)
        remote(pair_send.at[layer], pair_recv.at[layer], base, (dp, 2 * y + 1 - core, tm))

    def sums_y(layer, base):
        received(pair_recv.at[layer], base)
        lane = lax.broadcasted_iota(jnp.int32, (1, 128), 1)

        def fill(i, _):
            for j in range(4):
                def part(at):
                    where = pl.ds(at * 128, 128)
                    return total[2 * i + core, :, where] + pair_recv[layer, i, :, where].astype(F32)

                a, b, c, o = part(3 * j), part(3 * j + 1), part(3 * j + 2), part(12 + j)
                turn = lambda v, by: pltpu.roll(v, by, 1)
                y_send[layer, i, 4 * j] = jnp.where(lane < 96, a, turn(o, 96)).astype(BF)
                y_send[layer, i, 4 * j + 1] = jnp.where(
                    lane < 32, turn(a, 32), jnp.where(lane < 96, turn(b, 32), turn(o, 64))
                ).astype(BF)
                y_send[layer, i, 4 * j + 2] = jnp.where(
                    lane < 64, turn(b, 64), jnp.where(lane < 96, turn(c, 64), turn(o, 32))
                ).astype(BF)
                y_send[layer, i, 4 * j + 3] = jnp.where(lane < 96, turn(c, 96), o).astype(BF)
            return 0

        lax.fori_loop(0, 4, fill, 0)

        def send(i, _):
            p = lax.rem(y + i, 4)
            remote(y_send.at[layer, p], y_recv.at[layer, y], base + 1, (dp, 2 * p + core, tm))
            return 0

        lax.fori_loop(1, 4, send, 0)
        y_recv[layer, y] = y_send[layer, y]

    def sums_x(layer, base):
        received(y_recv.at[layer, pl.ds(0, 3)], base + 1)

        def add(i, _):
            value = y_recv[layer, 0, i].astype(F32)
            for j in range(1, 4):
                value = value + y_recv[layer, j, i].astype(F32)
            x_send[layer, lax.rem(i, 4), i // 4] = value.astype(BF)
            return 0

        lax.fori_loop(0, 16, add, 0)

        def send(i, _):
            p = lax.rem(x_at + i, 4)
            remote(x_send.at[layer, p], x_recv.at[layer, x_at], base + 2, (dp, station, z_hi * 4 + p))
            return 0

        lax.fori_loop(1, 4, send, 0)
        x_recv[layer, x_at] = x_send[layer, x_at]

    def sums_z(layer, base):
        received(x_recv.at[layer, pl.ds(0, 3)], base + 2)
        value = x_recv[layer, 0].astype(F32)
        for j in range(1, 4):
            value = value + x_recv[layer, j].astype(F32)
        z_send[layer] = value.astype(BF)
        mine = 2 * z_hi + dp

        def send(i, _):
            p = lax.rem(mine + i, 8)
            remote(
                z_send.at[layer, p // 2], z_recv.at[layer, mine], base + 3,
                (lax.rem(p, 2), station, (p // 2) * 4 + x_at),
            )
            return 0

        lax.fori_loop(1, 8, send, 0)
        z_recv[layer, mine] = z_send[layer, z_hi]

    def sums_end(layer, base, qkv_ref, out_ref):
        received(z_recv.at[layer, pl.ds(0, 7)], base + 3)
        value = z_recv[layer, 0].astype(F32)
        for j in range(1, 8):
            value = value + z_recv[layer, j].astype(F32)
        qkv_ref[...] = value[:, 0:96].astype(BF)
        out_ref[...] = pltpu.roll(value, 32, 1)[:, 0:32].astype(BF)

    sums_begin(1, R_TIME, ups_t[...])
    sums_y(1, R_TIME)

    received(gmid_recv.at[pl.ds(0, PEERS - 1)], R_GMID)

    def put_gmid(k, c, value):
        ups_s[128 * k : 128 * k + 128, 128 * c : 128 * c + 128] = value.astype(BF)

    unpack(gmid_recv, wide, put_gmid)
    grad_att[...] = nt(ups_s[...], wo_s[...]).astype(BF)

    def station_loop(step, _):
        backward_step(step, joined_s, probs, att_t.at[0], grad_att, grad_joined, grad_q_t, False)
        return 0

    lax.fori_loop(0, 2 * PAIRS, station_loop, 0, unroll=8)
    grad_joined[:, 0:WIDTH] = grad_q_t[...].T
    sums_x(1, R_TIME)
    grad_acted = nt(grad_joined[...], wq_s[...])
    x_value = xs[...].reshape(TOKENS, WIDTH).astype(F32)
    inverse_s = lax.rsqrt(jnp.mean(x_value * x_value, axis=1, keepdims=True) + EPSILON)
    gain_sum_s, grad_in = norm_backward(
        x_value, inverse_s, gain_s, grad_acted, ups_s[...].astype(F32)
    )
    gin_send[...] = grad_in.astype(BF).reshape(2, 2, 8, 16, WIDTH)

    def send_gin(i, _):
        p = lax.rem(station + i, 8)
        remote(gin_send.at[:, :, p], gin_recv.at[station], R_GIN, (dp, p, tm))
        return 0

    lax.fori_loop(1, 8, send_gin, 0)
    gin_recv[station] = gin_send[:, :, station]

    for c in range(4):
        gain_send[0, c : c + 1, :] = gain_sum_s[:, 128 * c : 128 * c + 128]
        gain_send[0, 4 + c : 5 + c, :] = gain_sum_t[:, 128 * c : 128 * c + 128]

    def send_gain_s(i, _):
        p = lax.rem(station + i, 8)
        remote(gain_send.at[0], gain_s_recv.at[station], R_GAIN_S, (dp, p, tm))
        return 0

    lax.fori_loop(1, 8, send_gain_s, 0)
    gain_s_recv[station] = gain_send[0]

    sums_begin(0, R_STATION, ups_s[...])
    sums_z(1, R_TIME)
    sums_y(0, R_STATION)

    received(gain_s_recv.at[pl.ds(0, 7)], R_GAIN_S)
    value = gain_s_recv[0]
    for j in range(1, 8):
        value = value + gain_s_recv[j]
    gain_send[1] = value

    def send_gain_x(i, _):
        p = lax.rem(x_at + i, 4)
        remote(gain_send.at[1], gain_x_recv.at[x_at], R_GAIN_X, (dp, station, z_hi * 4 + p))
        return 0

    lax.fori_loop(1, 4, send_gain_x, 0)
    gain_x_recv[x_at] = value

    sums_end(1, R_TIME, gq_t_ref, go_t_ref)

    received(gin_recv.at[pl.ds(0, 7)], R_GIN)
    for s in range(8):
        for e in range(2):
            for st in range(2):
                for c in range(4):
                    fine[c, pl.ds(st * 16 + 2 * s + e, 16, stride=32), :] = gin_recv[
                        s, e, st, :, 128 * c : 128 * c + 128
                    ].astype(F32)
    for c in range(4):
        gin_ref[:, :, 128 * c : 128 * c + 128] = fine[c].astype(BF).reshape(32, 16, 128)

    received(gain_x_recv.at[pl.ds(0, 3)], R_GAIN_X)
    value = gain_x_recv[0]
    for j in range(1, 4):
        value = value + gain_x_recv[j]
    gain_send[2] = value
    mine = 2 * z_hi + dp

    def send_gain_z(i, _):
        p = lax.rem(mine + i, 8)
        remote(
            gain_send.at[2], gain_z_recv.at[mine], R_GAIN_Z,
            (lax.rem(p, 2), station, (p // 2) * 4 + x_at),
        )
        return 0

    lax.fori_loop(1, 8, send_gain_z, 0)
    gain_z_recv[mine] = value

    sums_x(0, R_STATION)
    received(gain_z_recv.at[pl.ds(0, 7)], R_GAIN_Z)
    value = gain_z_recv[0]
    for j in range(1, 8):
        value = value + gain_z_recv[j]
    for c in range(4):
        gg_s_ref[:, 128 * c : 128 * c + 128] = value[c : c + 1]
        gg_t_ref[:, 128 * c : 128 * c + 128] = value[4 + c : 5 + c]
    sums_z(0, R_STATION)
    sums_end(0, R_STATION, gq_s_ref, go_s_ref)

    sent(in_send.at[pl.ds(0, 7)], R_IN)
    sent(cot_recv.at[:, pl.ds(0, 15)], R_COT)
    sent(mid_send.at[pl.ds(0, PEERS - 1)], R_MID)
    sent(gmid_send.at[pl.ds(0, PEERS - 1)], R_GMID)
    sent(gin_recv.at[pl.ds(0, 7)], R_GIN)
    sent(gain_s_recv.at[pl.ds(0, 7)], R_GAIN_S)
    sent(gain_x_recv.at[pl.ds(0, 3)], R_GAIN_X)
    sent(gain_z_recv.at[pl.ds(0, 7)], R_GAIN_Z)
    for layer, base in ((1, R_TIME), (0, R_STATION)):
        sent(pair_send.at[layer], base)
        sent(y_recv.at[layer, pl.ds(0, 3)], base + 1)
        sent(x_recv.at[layer, pl.ds(0, 3)], base + 2)
        sent(z_recv.at[layer, pl.ds(0, 7)], base + 3)


def local(inputs, cotangent, station_gain, station_qkv, station_out, time_gain, time_qkv, time_out):
    any_space = pl.BlockSpec(memory_space=pl.ANY)
    vmem = pl.BlockSpec(memory_space=pltpu.VMEM)
    shape = jax.ShapeDtypeStruct
    results = pl.pallas_call(
        kernel,
        out_shape=(
            shape((32, 16, WIDTH), BF),
            shape((64, 96), BF), shape((64, 32), BF), shape((1, WIDTH), F32),
            shape((64, 96), BF), shape((64, 32), BF), shape((1, WIDTH), F32),
        ),
        in_specs=[any_space, any_space, vmem, any_space, any_space, vmem, any_space, any_space],
        out_specs=[vmem] * 7,
        scratch_shapes=[
            pltpu.VMEM((32, 16, WIDTH), BF),
            pltpu.VMEM((4, TOKENS, 128), F32),
            pltpu.VMEM((PEERS * 16, 128), F32),
            pltpu.VMEM((8, 2, 2, 16, WIDTH), BF),
            pltpu.VMEM((2, 2, 8, 16, WIDTH), BF),
            pltpu.VMEM((2, 16, 16, WIDTH), BF),
            pltpu.VMEM((TOKENS, WIDTH), BF),
            pltpu.VMEM((WIDTH, 3 * WIDTH), BF),
            pltpu.VMEM((WIDTH, WIDTH), BF),
            pltpu.VMEM((WIDTH, 3 * WIDTH), BF),
            pltpu.VMEM((WIDTH, WIDTH), BF),
            pltpu.VMEM((2, TOKENS, WIDTH), BF),
            pltpu.VMEM((TOKENS, 3 * WIDTH), BF),
            pltpu.VMEM((TOKENS, 3 * WIDTH), BF),
            pltpu.VMEM((16, SEQ, SEQ), F32),
            pltpu.VMEM((2, WIDTH, TOKENS), BF),
            pltpu.VMEM((TOKENS, WIDTH), BF),
            pltpu.VMEM((TOKENS, 3 * WIDTH), BF),
            pltpu.VMEM((WIDTH, TOKENS), BF),
            pltpu.VMEM((2, WIDTH, TOKENS), BF),
            pltpu.VMEM((PEERS, 16, 128), BF),
            pltpu.VMEM((PEERS, 16, 128), BF),
            pltpu.VMEM((TOKENS, WIDTH), F32),
            pltpu.VMEM((PEERS, 16, 128), BF),
            pltpu.VMEM((PEERS, 16, 128), BF),
            pltpu.VMEM((TOKENS, WIDTH), BF),
            pltpu.VMEM((2, 2, 8, 16, WIDTH), BF),
            pltpu.VMEM((8, 2, 2, 16, WIDTH), BF),
            pltpu.VMEM((8, 64, 4 * WIDTH), F32),
            pltpu.VMEM((2, 4, 64, 4 * WIDTH), BF),
            pltpu.VMEM((2, 4, 64, 4 * WIDTH), BF),
            pltpu.VMEM((2, 4, 16, 64, 128), BF),
            pltpu.VMEM((2, 4, 16, 64, 128), BF),
            pltpu.VMEM((2, 4, 4, 64, 128), BF),
            pltpu.VMEM((2, 4, 4, 64, 128), BF),
            pltpu.VMEM((2, 4, 64, 128), BF),
            pltpu.VMEM((2, 8, 64, 128), BF),
            pltpu.VMEM((3, 8, 128), F32),
            pltpu.VMEM((8, 8, 128), F32),
            pltpu.VMEM((4, 8, 128), F32),
            pltpu.VMEM((8, 8, 128), F32),
            pltpu.SemaphoreType.DMA((N_SEMS,)),
            pltpu.SemaphoreType.DMA((N_SEMS,)),
            pltpu.SemaphoreType.DMA((6,)),
        ],
        compiler_params=pltpu.CompilerParams(
            collective_id=0, has_side_effects=True, vmem_limit_bytes=60 * 2**20
        ),
    )(
        inputs.reshape(32, 16, WIDTH), cotangent.reshape(32, 16, WIDTH),
        station_gain.reshape(1, WIDTH), station_qkv, station_out,
        time_gain.reshape(1, WIDTH), time_qkv, time_out,
    )
    grad_in, qkv_s, out_s, gain_s, qkv_t, out_t, gain_t = results
    return (
        grad_in.reshape(inputs.shape),
        qkv_s, out_s, gain_s.reshape(WIDTH), qkv_t, out_t, gain_t.reshape(WIDTH),
    )


def solution(mesh):
    rows = P("dp", "station", "tm", None)
    split = P("station", "tm")
    return jax.shard_map(
        local,
        mesh=mesh,
        in_specs=(rows, rows, P(), P(), P(), P(), P(), P()),
        out_specs=(rows, split, split, P(), split, split, P()),
        check_vma=False,
    )
```

```python
import functools

import jax
import jax.numpy as jnp
from jax import lax
from jax.experimental import pallas as pl
from jax.experimental.pallas import tpu as pltpu
from jax.sharding import PartitionSpec as P

MESH = pl.DeviceIdType.MESH
BF = jnp.bfloat16
F32 = jnp.float32
EPSILON = 1e-05
WIDTH = 512
TOKENS = 512
SEQ = 256
PAIRS = 4
PEERS = 128

R_IN, R_COT, R_GIN, R_GAIN_S, R_GAIN_X, R_GAIN_Z, R_MID, R_GMID, R_TIME, R_STATION = (
    0, 1, 2, 3, 4, 5, 6, 8, 10, 16,
)
PAIR, FIRST_Y, FIRST_X, SECOND_X, SECOND_Y, THIRD = range(6)
N_SEMS = 22
L_X, L_COT, L_WQS, L_WOS, L_WQT, L_WOT = range(6)
CHUNK = 128


def nn(a, b):
    return jnp.dot(a, b, preferred_element_type=F32)


def nt(a, b):
    return lax.dot_general(a, b, (((1,), (1,)), ((), ())), preferred_element_type=F32)


def tn(a, b):
    return lax.dot_general(a, b, (((0,), (0,)), ((), ())), preferred_element_type=F32)


def columns(pair, base=0):
    return slice(base + pair * 128, base + pair * 128 + 128)


def half_masks(value):
    lane = lax.broadcasted_iota(jnp.int32, (1, 128), 1)
    first = jnp.where(lane < 64, value, 0.0).astype(BF)
    second = jnp.where(lane < 64, 0.0, value).astype(BF)
    return first, second


def stacked(block, masks):
    return jnp.concatenate([block * masks[0], block * masks[1]], axis=0)


def under(block):
    return jnp.concatenate([block[:, :CHUNK], block[:, CHUNK:]], axis=0)


def softmax_t(scores):
    expon = jnp.exp(scores)
    total = jnp.sum(expon, axis=0, keepdims=True)
    shrink = jnp.where(total > 1.0, 0.25, 1.0)
    return (expon * shrink) * (1.0 / (total * shrink))


def forward_part(seq, pair, part, joined, probs, attended):
    rows = slice(seq * SEQ, seq * SEQ + SEQ)
    own = slice(seq * SEQ + part * CHUNK, seq * SEQ + part * CHUNK + CHUNK)
    queries = stacked(joined[own, columns(pair)], half_masks(0.125))
    values = stacked(joined[rows, columns(pair, 2 * WIDTH)], half_masks(1.0))
    p = softmax_t(nt(joined[rows, columns(pair, WIDTH)], queries))
    probs[seq * PAIRS + pair, :, part * 2 * CHUNK : part * 2 * CHUNK + 2 * CHUNK] = p
    attended[own, columns(pair)] = tn(under(p.astype(BF)), values).astype(BF)


def backward_step(seq, pair, joined, probs, attended, grad_att, grad_joined):
    rows = slice(seq * SEQ, seq * SEQ + SEQ)
    eighths = half_masks(0.125)
    ones = half_masks(1.0)
    keys = joined[rows, columns(pair, WIDTH)]
    values = joined[rows, columns(pair, 2 * WIDTH)]
    key_rows = stacked(keys, eighths)
    if probs is None:
        value_rows = stacked(values, ones)
    qs, us, p_halves, grad_ss = [], [], [], []
    for part in range(SEQ // CHUNK):
        own = slice(seq * SEQ + part * CHUNK, seq * SEQ + part * CHUNK + CHUNK)
        q = stacked(joined[own, columns(pair)], eighths)
        u = stacked(grad_att[own, columns(pair)], ones)
        if probs is None:
            p = softmax_t(nt(keys, q))
        else:
            p = probs[seq * PAIRS + pair, :, part * 2 * CHUNK : part * 2 * CHUNK + 2 * CHUNK]
        p_half = p.astype(BF)
        if probs is None:
            attended[own, columns(pair)] = tn(under(p_half), value_rows).astype(BF)
        grad_p = nt(values, u)
        dot = jnp.sum(grad_p * p, axis=0, keepdims=True)
        grad_s = (p * (grad_p - dot)).astype(BF)
        grad_joined[own, columns(pair)] = tn(under(grad_s), key_rows).astype(BF)
        qs.append(q)
        us.append(u)
        p_halves.append(p_half)
        grad_ss.append(grad_s)
    join = jnp.concatenate
    grad_joined[rows, columns(pair, WIDTH)] = nn(join(grad_ss, axis=1), join(qs, axis=0)).astype(BF)
    grad_joined[rows, columns(pair, 2 * WIDTH)] = nn(
        join(p_halves, axis=1), join(us, axis=0)
    ).astype(BF)


def normalise(x, gain):
    inverse = lax.rsqrt(jnp.mean(x * x, axis=1, keepdims=True) + EPSILON)
    normed = x * inverse
    return inverse, (normed * gain).astype(BF)


def norm_backward(x, inverse, gain, grad_acted, upstream):
    normed = x * inverse
    grad_gain = jnp.sum(grad_acted * normed, axis=0, keepdims=True)
    grad_normed = grad_acted * gain
    mean = jnp.mean(grad_normed * normed, axis=1, keepdims=True)
    return grad_gain, upstream + inverse * (grad_normed - normed * mean)


def part_rows(ref, part):
    return jnp.concatenate([ref[part * 128 : part * 128 + 128], ref[256 + part * 128 : 384 + part * 128]], axis=0)


def put_rows(ref, part, value):
    ref[part * 128 : part * 128 + 128] = value[0:128]
    ref[256 + part * 128 : 384 + part * 128] = value[128:256]


def place(a, b, epoch_first):
    return a * 2 + b if epoch_first else b * 2 + a


def pack(value, part, epoch_first, wide, send):
    for a in range(2):
        for b in range(2):
            block = value[a * 128 + b * 64 : a * 128 + b * 64 + 64]
            for c in range(4):
                wide[
                    pl.ds(part * 1024 + c * 4 + place(a, b, epoch_first), 64, stride=16), :
                ] = block[:, 128 * c : 128 * c + 128]
    send[part] = wide[part * 1024 : part * 1024 + 1024].astype(BF).reshape(64, 16, 128)


def unpack(recv, part, epoch_first, wide, target):
    wide[part * 1024 : part * 1024 + 1024] = recv[part].reshape(1024, 128).astype(F32)
    for a in range(2):
        for b in range(2):
            row = a * 256 + part * 128 + b * 64
            for c in range(4):
                target[row : row + 64, 128 * c : 128 * c + 128] = wide[
                    pl.ds(part * 1024 + c * 4 + place(a, b, epoch_first), 64, stride=16), :
                ].astype(target.dtype)


def kernel(
    x_hbm, cot_hbm, gain_s_ref, wq_s_hbm, wo_s_hbm, gain_t_ref, wq_t_hbm, wo_t_hbm,
    gin_ref, sums_ref, gains_ref,
    x_raw, fine, wide, in_send, xs, cot_recv, ups_t, wq_s, wo_s, wq_t, wo_t,
    acted, joined_s, joined_t, probs, attended, grad_att, grad_joined, acted_t, att_t,
    mid_send, mid_recv, xt, gmid_send, gmid_recv, ups_s, gin_send, gin_recv,
    total, pair_send, pair_recv, y_send, y_recv, x1_send, x1_recv,
    xb_send, xb_recv, yb_send, yb_recv, z_send, z_recv,
    gain_send, gain_s_recv, gain_x_recv, gain_z_recv,
    send_sems, recv_sems, local_sems,
):
    dp, station, tm = lax.axis_index("dp"), lax.axis_index("station"), lax.axis_index("tm")
    y, core = station // 2, lax.rem(station, 2)
    z_hi, x_at = tm // 4, lax.rem(tm, 4)
    spot = y * 16 + tm

    def local_copy(source, target, sem):
        return pltpu.make_async_copy(source, target, local_sems.at[sem])

    def remote(source, target, sem, device):
        pltpu.make_async_remote_copy(
            src_ref=source, dst_ref=target, send_sem=send_sems.at[sem],
            recv_sem=recv_sems.at[sem], device_id=device, device_id_type=MESH,
        ).start()

    def received(ref, sem):
        pltpu.make_async_copy(ref, ref, recv_sems.at[sem]).wait()

    def sent(ref, sem):
        pltpu.make_async_copy(ref, ref, send_sems.at[sem]).wait()

    def each(first, last, action):
        def step(i, _):
            action(i)
            return 0

        lax.fori_loop(first, last, step, 0)

    loads = [
        local_copy(x_hbm, x_raw, L_X),
        local_copy(wq_s_hbm, wq_s, L_WQS),
        local_copy(wo_s_hbm, wo_s, L_WOS),
        local_copy(cot_hbm.at[pl.ds(2 * tm, 2)], cot_recv.at[:, tm], L_COT),
        local_copy(wq_t_hbm, wq_t, L_WQT),
        local_copy(wo_t_hbm, wo_t, L_WOT),
    ]
    for load in loads:
        load.start()

    barrier = pltpu.get_barrier_semaphore()

    def greet(device):
        pl.semaphore_signal(barrier, inc=1, device_id=device, device_id_type=MESH)

    each(1, 8, lambda i: greet((dp, lax.rem(station + i, 8), tm)))
    each(1, 16, lambda i: greet((dp, station, lax.rem(tm + i, 16))))
    each(0, 4, lambda i: greet((1 - dp, station, i * 4 + x_at)))

    loads[0].wait()
    for c in range(4):
        fine[c] = x_raw[:, :, 128 * c : 128 * c + 128].astype(F32).reshape(TOKENS, 128)
    for s in range(8):
        for e in range(2):
            for st in range(2):
                for c in range(4):
                    in_send[s, e, st, :, 128 * c : 128 * c + 128] = fine[
                        c, pl.ds(st * 16 + 2 * s + e, 16, stride=32), :
                    ].astype(BF)
    pl.semaphore_wait(barrier, 26)

    def send_in(i):
        p = lax.rem(station + i, 8)
        remote(
            in_send.at[p], xs.at[:, lax.rem(station + p, 2), :, y], R_IN, (dp, p, tm)
        )

    def send_cot(i):
        p = lax.rem(tm + i, 16)
        remote(cot_hbm.at[pl.ds(2 * p, 2)], cot_recv.at[:, tm], R_COT, (dp, station, p))

    each(1, 8, send_in)
    each(1, 16, send_cot)
    xs[:, 0, :, y] = in_send[station]

    received(in_send.at[pl.ds(0, 7)], R_IN)
    loads[1].wait()
    gain_s = gain_s_ref[...]
    _, acted_value = normalise(xs[...].reshape(TOKENS, WIDTH).astype(F32), gain_s)
    acted[0] = acted_value
    joined_s[...] = nn(acted_value, wq_s[...]).astype(BF)
    loads[2].wait()

    def send_parts(send, recv, sem, part):
        other = lax.rem(core + part, 2)

        def action(i):
            p = lax.rem(spot + i, 64)
            remote(
                send.at[part, p], recv.at[part, spot], sem + part,
                (dp, 2 * (p // 16) + other, lax.rem(p, 16)),
            )

        each(1 - part, 64, action)

    for part in range(2):
        for seq in range(2):
            for pair in range(PAIRS):
                forward_part(seq, pair, part, joined_s, probs, attended.at[0])
        x_part = jnp.concatenate(
            [xs[0, part].reshape(128, WIDTH), xs[1, part].reshape(128, WIDTH)], axis=0
        )
        mid = x_part.astype(F32) + nn(part_rows(attended.at[0], part), wo_s[...])
        pack(mid, part, True, wide, mid_send)
        send_parts(mid_send, mid_recv, R_MID, part)
    mid_recv[0, spot] = mid_send[0, spot]

    loads[3].wait()
    received(cot_recv.at[:, pl.ds(0, 15)], R_COT)
    for c in range(4):
        fine[c] = cot_recv[:, :, :, 128 * c : 128 * c + 128].astype(F32).reshape(TOKENS, 128)
    for s in range(8):
        part = lax.rem(core + s, 2)
        for st in range(2):
            for e in range(2):
                for c in range(4):
                    ups_t[st, part, e, s // 2, :, 128 * c : 128 * c + 128] = fine[
                        c, pl.ds(st * 256 + 2 * s + e, 16, stride=16), :
                    ].astype(BF)
    loads[4].wait()
    loads[5].wait()
    upstream_t = ups_t[...].reshape(TOKENS, WIDTH)
    grad_att[...] = nt(upstream_t, wo_t[...]).astype(BF)
    acted_t[0] = acted[0].T.reshape(4, 2, 64, TOKENS)
    att_t[0] = attended[0].T.reshape(4, 2, 64, TOKENS)

    gain_t = gain_t_ref[...]
    for part in range(2):
        received(mid_recv.at[part, pl.ds(0, 63 + part)], R_MID + part)
        unpack(mid_recv, part, False, wide, xt)
        _, acted_value = normalise(part_rows(xt, part), gain_t)
        put_rows(acted.at[1], part, acted_value)
        put_rows(joined_t, part, nn(acted_value, wq_t[...]).astype(BF))

    for seq in range(2):
        for pair in range(PAIRS):
            backward_step(seq, pair, joined_t, None, attended.at[1], grad_att, grad_joined)
    gain_sum_t = None
    for part in range(2):
        x_value = part_rows(xt, part)
        inverse = lax.rsqrt(jnp.mean(x_value * x_value, axis=1, keepdims=True) + EPSILON)
        grad_acted = nt(part_rows(grad_joined, part), wq_t[...])
        up_part = jnp.concatenate(
            [ups_t[0, part].reshape(128, WIDTH), ups_t[1, part].reshape(128, WIDTH)], axis=0
        )
        gain_part, grad_mid = norm_backward(
            x_value, inverse, gain_t, grad_acted, up_part.astype(F32)
        )
        gain_sum_t = gain_part if gain_sum_t is None else gain_sum_t + gain_part
        pack(grad_mid, part, False, wide, gmid_send)
        send_parts(gmid_send, gmid_recv, R_GMID, part)
    gmid_recv[0, spot] = gmid_send[0, spot]

    def products(layer, who, upstream):
        left = acted_t[layer, :, who].reshape(256, TOKENS)
        left_out = att_t[layer, :, who].reshape(256, TOKENS)
        return (
            nn(left, grad_joined[...]).reshape(4, 64, 3 * WIDTH),
            nn(left_out, upstream).reshape(4, 64, WIDTH),
        )

    def sums_send(layer, base, upstream):
        qkv, out = products(layer, 1 - core, upstream)
        pair_send[layer, :, :, 0 : 3 * WIDTH] = qkv.astype(BF)
        pair_send[layer, :, :, 3 * WIDTH :] = out.astype(BF)
        remote(pair_send.at[layer], pair_recv.at[layer], base + PAIR, (dp, 2 * y + 1 - core, tm))

    def sums_own(layer, upstream):
        qkv, out = products(layer, core, upstream)
        total[:, :, 0 : 3 * WIDTH] = qkv
        total[:, :, 3 * WIDTH :] = out

    def sums_first(layer, base):
        received(pair_recv.at[layer], base + PAIR)
        lane = lax.broadcasted_iota(jnp.int32, (1, 128), 1)

        def fill(i):
            def put(t, value):
                value = value.astype(BF)
                y_send[layer, i, t] = value[0:32]
                x1_send[layer, t % 4, i, t // 4] = value[32:64]

            for j in range(4):
                def piece(at):
                    where = slice(at * 128, at * 128 + 128)
                    return total[i, :, where] + pair_recv[layer, i, :, where].astype(F32)

                a, b, c, o = piece(3 * j), piece(3 * j + 1), piece(3 * j + 2), piece(12 + j)
                turn = lambda v, by: pltpu.roll(v, by, 1)
                put(4 * j, jnp.where(lane < 96, a, turn(o, 96)))
                put(4 * j + 1, jnp.where(lane < 32, turn(a, 32), jnp.where(lane < 96, turn(b, 32), turn(o, 64))))
                put(4 * j + 2, jnp.where(lane < 64, turn(b, 64), jnp.where(lane < 96, turn(c, 64), turn(o, 32))))
                put(4 * j + 3, jnp.where(lane < 96, turn(c, 96), o))

        each(0, 4, fill)

        def send_x(i):
            p = lax.rem(x_at + i, 4)
            remote(
                x1_send.at[layer, p], x1_recv.at[layer, x_at], base + FIRST_X,
                (dp, station, z_hi * 4 + p),
            )

        def send_y(i):
            p = lax.rem(y + i, 4)
            remote(
                y_send.at[layer, p], y_recv.at[layer, y], base + FIRST_Y, (dp, 2 * p + core, tm)
            )

        each(1, 4, send_x)
        each(1, 4, send_y)
        y_recv[layer, y] = y_send[layer, y]
        x1_recv[layer, x_at] = x1_send[layer, x_at]

    def sums_second(layer, base):
        received(x1_recv.at[layer, pl.ds(0, 3)], base + FIRST_X)

        def add_x(i):
            value = x1_recv[layer, 0, i].astype(F32)
            for j in range(1, 4):
                value = value + x1_recv[layer, j, i].astype(F32)
            yb_send[layer, i] = value.astype(BF)

        each(0, 4, add_x)

        def send_y(i):
            p = lax.rem(y + i, 4)
            remote(
                yb_send.at[layer, p], yb_recv.at[layer, y], base + SECOND_Y, (dp, 2 * p + core, tm)
            )

        each(1, 4, send_y)
        yb_recv[layer, y] = yb_send[layer, y]

        received(y_recv.at[layer, pl.ds(0, 3)], base + FIRST_Y)

        def add_y(i):
            for at in range(4):
                value = y_recv[layer, 0, 4 * i + at].astype(F32)
                for j in range(1, 4):
                    value = value + y_recv[layer, j, 4 * i + at].astype(F32)
                xb_send[layer, at, i] = value.astype(BF)

        each(0, 4, add_y)

        def send_x(i):
            p = lax.rem(x_at + i, 4)
            remote(
                xb_send.at[layer, p], xb_recv.at[layer, x_at], base + SECOND_X,
                (dp, station, z_hi * 4 + p),
            )

        each(1, 4, send_x)
        xb_recv[layer, x_at] = xb_send[layer, x_at]

    def sums_third(layer, base):
        received(yb_recv.at[layer, pl.ds(0, 3)], base + SECOND_Y)
        received(xb_recv.at[layer, pl.ds(0, 3)], base + SECOND_X)
        low, high = xb_recv[layer, 0].astype(F32), yb_recv[layer, 0].astype(F32)
        for j in range(1, 4):
            low = low + xb_recv[layer, j].astype(F32)
            high = high + yb_recv[layer, j].astype(F32)
        z_send[layer, :, 0:32] = low.astype(BF)
        z_send[layer, :, 32:64] = high.astype(BF)
        mine = 2 * z_hi + dp

        def send(i):
            p = lax.rem(mine + i, 8)
            remote(
                z_send.at[layer, p // 2], z_recv.at[layer, mine], base + THIRD,
                (lax.rem(p, 2), station, (p // 2) * 4 + x_at),
            )

        each(1, 8, send)
        z_recv[layer, mine] = z_send[layer, z_hi]

    def sums_end(layer, base):
        received(z_recv.at[layer, pl.ds(0, 7)], base + THIRD)
        value = z_recv[layer, 0].astype(F32)
        for j in range(1, 8):
            value = value + z_recv[layer, j].astype(F32)
        sums_ref[layer] = value.astype(BF)

    acted_t[1] = acted[1].T.reshape(4, 2, 64, TOKENS)
    att_t[1] = attended[1].T.reshape(4, 2, 64, TOKENS)
    sums_send(1, R_TIME, upstream_t)
    sums_own(1, upstream_t)
    sums_first(1, R_TIME)

    for part in range(2):
        received(gmid_recv.at[part, pl.ds(0, 63 + part)], R_GMID + part)
        unpack(gmid_recv, part, True, wide, ups_s)
        put_rows(grad_att, part, nt(part_rows(ups_s, part), wo_s[...]).astype(BF))
    for seq in range(2):
        for pair in range(PAIRS):
            backward_step(seq, pair, joined_s, probs, None, grad_att, grad_joined)
    sums_send(0, R_STATION, ups_s[...])
    sums_second(1, R_TIME)
    grad_acted = nt(grad_joined[...], wq_s[...])
    x_value = xs[...].reshape(TOKENS, WIDTH).astype(F32)
    inverse_s = lax.rsqrt(jnp.mean(x_value * x_value, axis=1, keepdims=True) + EPSILON)
    gain_sum_s, grad_in = norm_backward(
        x_value, inverse_s, gain_s, grad_acted, ups_s[...].astype(F32)
    )
    gin_send[...] = grad_in.astype(BF).reshape(2, 2, 2, 4, 16, WIDTH)

    def send_gin(i):
        p = lax.rem(station + i, 8)
        remote(
            gin_send.at[:, lax.rem(station + p, 2), :, p // 2], gin_recv.at[station], R_GIN,
            (dp, p, tm),
        )

    each(1, 8, send_gin)
    gin_recv[station] = gin_send[:, 0, :, y]

    for c in range(4):
        gain_send[0, c : c + 1, :] = gain_sum_s[:, 128 * c : 128 * c + 128]
        gain_send[0, 4 + c : 5 + c, :] = gain_sum_t[:, 128 * c : 128 * c + 128]

    def send_gain_s(i):
        p = lax.rem(station + i, 8)
        remote(gain_send.at[0], gain_s_recv.at[station], R_GAIN_S, (dp, p, tm))

    each(1, 8, send_gain_s)
    gain_s_recv[station] = gain_send[0]

    sums_own(0, ups_s[...])
    sums_first(0, R_STATION)
    sums_third(1, R_TIME)

    received(gain_s_recv.at[pl.ds(0, 7)], R_GAIN_S)
    value = gain_s_recv[0]
    for j in range(1, 8):
        value = value + gain_s_recv[j]
    gain_send[1] = value

    def send_gain_x(i):
        p = lax.rem(x_at + i, 4)
        remote(gain_send.at[1], gain_x_recv.at[x_at], R_GAIN_X, (dp, station, z_hi * 4 + p))

    each(1, 4, send_gain_x)
    gain_x_recv[x_at] = value
    sums_end(1, R_TIME)

    received(gain_x_recv.at[pl.ds(0, 3)], R_GAIN_X)
    value = gain_x_recv[0]
    for j in range(1, 4):
        value = value + gain_x_recv[j]
    gain_send[2] = value
    mine = 2 * z_hi + dp

    def send_gain_z(i):
        p = lax.rem(mine + i, 8)
        remote(
            gain_send.at[2], gain_z_recv.at[mine], R_GAIN_Z,
            (lax.rem(p, 2), station, (p // 2) * 4 + x_at),
        )

    each(1, 8, send_gain_z)
    gain_z_recv[mine] = value

    sums_second(0, R_STATION)

    received(gin_recv.at[pl.ds(0, 7)], R_GIN)
    for s in range(8):
        for e in range(2):
            for st in range(2):
                for c in range(4):
                    fine[c, pl.ds(st * 16 + 2 * s + e, 16, stride=32), :] = gin_recv[
                        s, e, st, :, 128 * c : 128 * c + 128
                    ].astype(F32)
    for c in range(4):
        gin_ref[:, :, 128 * c : 128 * c + 128] = fine[c].astype(BF).reshape(32, 16, 128)

    sums_third(0, R_STATION)
    received(gain_z_recv.at[pl.ds(0, 7)], R_GAIN_Z)
    value = gain_z_recv[0]
    for j in range(1, 8):
        value = value + gain_z_recv[j]
    gains_ref[...] = value

    sent(in_send.at[pl.ds(0, 7)], R_IN)
    sent(cot_recv.at[:, pl.ds(0, 15)], R_COT)
    for part in range(2):
        sent(mid_send.at[part, pl.ds(0, 63 + part)], R_MID + part)
        sent(gmid_send.at[part, pl.ds(0, 63 + part)], R_GMID + part)
    sent(gin_recv.at[pl.ds(0, 7)], R_GIN)
    sent(gain_s_recv.at[pl.ds(0, 7)], R_GAIN_S)
    sent(gain_x_recv.at[pl.ds(0, 3)], R_GAIN_X)
    sent(gain_z_recv.at[pl.ds(0, 7)], R_GAIN_Z)
    for layer, base in ((1, R_TIME), (0, R_STATION)):
        sent(pair_send.at[layer], base + PAIR)
        sent(y_recv.at[layer, pl.ds(0, 3)], base + FIRST_Y)
        sent(x1_recv.at[layer, pl.ds(0, 3)], base + FIRST_X)
        sent(xb_recv.at[layer, pl.ds(0, 3)], base + SECOND_X)
        sent(yb_recv.at[layer, pl.ds(0, 3)], base + SECOND_Y)
        sent(z_recv.at[layer, pl.ds(0, 7)], base + THIRD)
    sums_end(0, R_STATION)


def deliver(gin, sums, gains, gin_ref, gq_s_ref, go_s_ref, gg_s_ref, gq_t_ref, go_t_ref, gg_t_ref):
    gin_ref[...] = gin[...]
    for layer, qkv_ref, out_ref in ((0, gq_s_ref, go_s_ref), (1, gq_t_ref, go_t_ref)):
        value = sums[layer].astype(F32)
        qkv_ref[...] = value[:, 0:96].astype(BF)
        out_ref[...] = pltpu.roll(value, 32, 1)[:, 0:32].astype(BF)
    for c in range(4):
        gg_s_ref[:, 128 * c : 128 * c + 128] = gains[c : c + 1]
        gg_t_ref[:, 128 * c : 128 * c + 128] = gains[4 + c : 5 + c]


def local(inputs, cotangent, station_gain, station_qkv, station_out, time_gain, time_qkv, time_out):
    any_space = pl.BlockSpec(memory_space=pl.ANY)
    vmem = pl.BlockSpec(memory_space=pltpu.VMEM)
    shape = jax.ShapeDtypeStruct
    merged = pl.pallas_call(
        kernel,
        out_shape=(shape((32, 16, WIDTH), BF), shape((2, 64, 128), BF), shape((8, 128), F32)),
        in_specs=[any_space, any_space, vmem, any_space, any_space, vmem, any_space, any_space],
        out_specs=[vmem] * 3,
        scratch_shapes=[
            pltpu.VMEM((32, 16, WIDTH), BF),
            pltpu.VMEM((4, TOKENS, 128), F32),
            pltpu.VMEM((PEERS * 16, 128), F32),
            pltpu.VMEM((8, 2, 2, 16, WIDTH), BF),
            pltpu.VMEM((2, 2, 2, 4, 16, WIDTH), BF),
            pltpu.VMEM((2, 16, 16, WIDTH), BF),
            pltpu.VMEM((2, 2, 2, 4, 16, WIDTH), BF),
            pltpu.VMEM((WIDTH, 3 * WIDTH), BF),
            pltpu.VMEM((WIDTH, WIDTH), BF),
            pltpu.VMEM((WIDTH, 3 * WIDTH), BF),
            pltpu.VMEM((WIDTH, WIDTH), BF),
            pltpu.VMEM((2, TOKENS, WIDTH), BF),
            pltpu.VMEM((TOKENS, 3 * WIDTH), BF),
            pltpu.VMEM((TOKENS, 3 * WIDTH), BF),
            pltpu.VMEM((8, SEQ, 2 * SEQ), F32),
            pltpu.VMEM((2, TOKENS, WIDTH), BF),
            pltpu.VMEM((TOKENS, WIDTH), BF),
            pltpu.VMEM((TOKENS, 3 * WIDTH), BF),
            pltpu.VMEM((2, 4, 2, 64, TOKENS), BF),
            pltpu.VMEM((2, 4, 2, 64, TOKENS), BF),
            pltpu.VMEM((2, 64, 16, 128), BF),
            pltpu.VMEM((2, 64, 16, 128), BF),
            pltpu.VMEM((TOKENS, WIDTH), F32),
            pltpu.VMEM((2, 64, 16, 128), BF),
            pltpu.VMEM((2, 64, 16, 128), BF),
            pltpu.VMEM((TOKENS, WIDTH), BF),
            pltpu.VMEM((2, 2, 2, 4, 16, WIDTH), BF),
            pltpu.VMEM((8, 2, 2, 16, WIDTH), BF),
            pltpu.VMEM((4, 64, 4 * WIDTH), F32),
            pltpu.VMEM((2, 4, 64, 4 * WIDTH), BF),
            pltpu.VMEM((2, 4, 64, 4 * WIDTH), BF),
            pltpu.VMEM((2, 4, 16, 32, 128), BF),
            pltpu.VMEM((2, 4, 16, 32, 128), BF),
            pltpu.VMEM((2, 4, 4, 4, 32, 128), BF),
            pltpu.VMEM((2, 4, 4, 4, 32, 128), BF),
            pltpu.VMEM((2, 4, 4, 32, 128), BF),
            pltpu.VMEM((2, 4, 4, 32, 128), BF),
            pltpu.VMEM((2, 4, 4, 32, 128), BF),
            pltpu.VMEM((2, 4, 4, 32, 128), BF),
            pltpu.VMEM((2, 4, 64, 128), BF),
            pltpu.VMEM((2, 8, 64, 128), BF),
            pltpu.VMEM((3, 8, 128), F32),
            pltpu.VMEM((8, 8, 128), F32),
            pltpu.VMEM((4, 8, 128), F32),
            pltpu.VMEM((8, 8, 128), F32),
            pltpu.SemaphoreType.DMA((N_SEMS,)),
            pltpu.SemaphoreType.DMA((N_SEMS,)),
            pltpu.SemaphoreType.DMA((6,)),
        ],
        compiler_params=pltpu.CompilerParams(
            collective_id=0, has_side_effects=True, vmem_limit_bytes=60 * 2**20
        ),
    )(
        inputs.reshape(32, 16, WIDTH), cotangent.reshape(32, 16, WIDTH),
        station_gain.reshape(1, WIDTH), station_qkv, station_out,
        time_gain.reshape(1, WIDTH), time_qkv, time_out,
    )
    grad_in, qkv_s, out_s, gain_s, qkv_t, out_t, gain_t = pl.pallas_call(
        deliver,
        out_shape=(
            shape((32, 16, WIDTH), BF),
            shape((64, 96), BF), shape((64, 32), BF), shape((1, WIDTH), F32),
            shape((64, 96), BF), shape((64, 32), BF), shape((1, WIDTH), F32),
        ),
        in_specs=[vmem] * 3,
        out_specs=[vmem] * 7,
    )(*merged)
    return (
        grad_in.reshape(inputs.shape),
        qkv_s, out_s, gain_s.reshape(WIDTH), qkv_t, out_t, gain_t.reshape(WIDTH),
    )


def solution(mesh):
    rows = P("dp", "station", "tm", None)
    split = P("station", "tm")
    return jax.shard_map(
        local,
        mesh=mesh,
        in_specs=(rows, rows, P(), P(), P(), P(), P(), P()),
        out_specs=(rows, split, split, P(), split, split, P()),
        check_vma=False,
    )
```

```python
import functools

import jax
import jax.numpy as jnp
from jax import lax
from jax.experimental import pallas as pl
from jax.experimental.pallas import tpu as pltpu
from jax.sharding import PartitionSpec as P

MESH = pl.DeviceIdType.MESH
BF = jnp.bfloat16
F32 = jnp.float32
EPSILON = 1e-05
WIDTH = 512
TOKENS = 512
SEQ = 256
PAIRS = 4
PEERS = 128

R_IN, R_COT, R_GIN, R_GAIN_S, R_GAIN_X, R_GAIN_Z, R_MID, R_GMID, R_TIME, R_STATION = (
    0, 1, 2, 3, 4, 5, 6, 8, 10, 16,
)
PAIR, FIRST_Y, FIRST_X, SECOND_X, SECOND_Y, THIRD = range(6)
FIRST_Z, Z_THEN_Y, Z_THEN_X = 6, 7, 8
N_SEMS = 25
L_X, L_COT, L_WQS, L_WOS, L_WQT, L_WOT, L_OUT = range(7)
CHUNK = 128


def nn(a, b):
    return jnp.dot(a, b, preferred_element_type=F32)


def nt(a, b):
    return lax.dot_general(a, b, (((1,), (1,)), ((), ())), preferred_element_type=F32)


def tn(a, b):
    return lax.dot_general(a, b, (((0,), (0,)), ((), ())), preferred_element_type=F32)


def columns(pair, base=0):
    return slice(base + pair * 128, base + pair * 128 + 128)


def half_masks(value):
    lane = lax.broadcasted_iota(jnp.int32, (1, 128), 1)
    first = jnp.where(lane < 64, value, 0.0).astype(BF)
    second = jnp.where(lane < 64, 0.0, value).astype(BF)
    return first, second


def stacked(block, masks):
    return jnp.concatenate([block * masks[0], block * masks[1]], axis=0)


def under(block):
    return jnp.concatenate([block[:, :CHUNK], block[:, CHUNK:]], axis=0)


def softmax_t(scores):
    expon = jnp.exp(scores)
    total = jnp.sum(expon, axis=0, keepdims=True)
    shrink = jnp.where(total > 1.0, 0.25, 1.0)
    return (expon * shrink) * (1.0 / (total * shrink))


def forward_part(seq, pair, part, joined, probs, attended):
    rows = slice(seq * SEQ, seq * SEQ + SEQ)
    own = slice(seq * SEQ + part * CHUNK, seq * SEQ + part * CHUNK + CHUNK)
    queries = stacked(joined[own, columns(pair)], half_masks(0.125))
    values = stacked(joined[rows, columns(pair, 2 * WIDTH)], half_masks(1.0))
    p = softmax_t(nt(joined[rows, columns(pair, WIDTH)], queries))
    probs[seq * PAIRS + pair, :, part * 2 * CHUNK : part * 2 * CHUNK + 2 * CHUNK] = p
    attended[own, columns(pair)] = tn(under(p.astype(BF)), values).astype(BF)


def backward_step(seq, pair, joined, probs, attended, grad_att, grad_joined):
    rows = slice(seq * SEQ, seq * SEQ + SEQ)
    eighths = half_masks(0.125)
    ones = half_masks(1.0)
    keys = joined[rows, columns(pair, WIDTH)]
    values = joined[rows, columns(pair, 2 * WIDTH)]
    key_rows = stacked(keys, eighths)
    if probs is None:
        value_rows = stacked(values, ones)
    qs, us, p_halves, grad_ss = [], [], [], []
    for part in range(SEQ // CHUNK):
        own = slice(seq * SEQ + part * CHUNK, seq * SEQ + part * CHUNK + CHUNK)
        q = stacked(joined[own, columns(pair)], eighths)
        u = stacked(grad_att[own, columns(pair)], ones)
        if probs is None:
            p = softmax_t(nt(keys, q))
        else:
            p = probs[seq * PAIRS + pair, :, part * 2 * CHUNK : part * 2 * CHUNK + 2 * CHUNK]
        p_half = p.astype(BF)
        if probs is None:
            attended[own, columns(pair)] = tn(under(p_half), value_rows).astype(BF)
        grad_p = nt(values, u)
        dot = jnp.sum(grad_p * p, axis=0, keepdims=True)
        grad_s = (p * (grad_p - dot)).astype(BF)
        grad_joined[own, columns(pair)] = tn(under(grad_s), key_rows).astype(BF)
        qs.append(q)
        us.append(u)
        p_halves.append(p_half)
        grad_ss.append(grad_s)
    join = jnp.concatenate
    grad_joined[rows, columns(pair, WIDTH)] = nn(join(grad_ss, axis=1), join(qs, axis=0)).astype(BF)
    grad_joined[rows, columns(pair, 2 * WIDTH)] = nn(
        join(p_halves, axis=1), join(us, axis=0)
    ).astype(BF)


def turn(value, by):
    return pltpu.roll(value, by, 1)


def slot(t, piece):
    lane = lax.broadcasted_iota(jnp.int32, (1, 128), 1)
    j, i = t // 4, t % 4
    parts = {
        0: ((3 * j, 0, 0, 96),),
        1: ((3 * j, 32, 0, 32), (3 * j + 1, 32, 32, 96)),
        2: ((3 * j + 1, 64, 0, 64), (3 * j + 2, 64, 64, 96)),
        3: ((3 * j + 2, 96, 0, 96),),
    }[i] + ((12 + j, 96 - 32 * i, 96, 128),)
    result = None
    for at, by, first, last in parts:
        value = piece(at)
        if value is None:
            continue
        if by:
            value = turn(value, by)
        inside = (lane >= first) & (lane < last)
        result = jnp.where(inside, value, 0.0 if result is None else result)
    return result


def normalise(x, gain):
    inverse = lax.rsqrt(jnp.mean(x * x, axis=1, keepdims=True) + EPSILON)
    normed = x * inverse
    return inverse, (normed * gain).astype(BF)


def norm_backward(x, inverse, gain, grad_acted, upstream):
    normed = x * inverse
    grad_gain = jnp.sum(grad_acted * normed, axis=0, keepdims=True)
    grad_normed = grad_acted * gain
    mean = jnp.mean(grad_normed * normed, axis=1, keepdims=True)
    return grad_gain, upstream + inverse * (grad_normed - normed * mean)


def part_rows(ref, part):
    return jnp.concatenate([ref[part * 128 : part * 128 + 128], ref[256 + part * 128 : 384 + part * 128]], axis=0)


def put_rows(ref, part, value):
    ref[part * 128 : part * 128 + 128] = value[0:128]
    ref[256 + part * 128 : 384 + part * 128] = value[128:256]


def place(a, b, epoch_first):
    return a * 2 + b if epoch_first else b * 2 + a


def pack(value, part, epoch_first, wide, send):
    for a in range(2):
        for b in range(2):
            block = value[a * 128 + b * 64 : a * 128 + b * 64 + 64]
            for c in range(4):
                wide[
                    pl.ds(part * 1024 + c * 4 + place(a, b, epoch_first), 64, stride=16), :
                ] = block[:, 128 * c : 128 * c + 128]
    send[part] = wide[part * 1024 : part * 1024 + 1024].astype(BF).reshape(64, 16, 128)


def unpack(recv, part, epoch_first, wide, target):
    wide[part * 1024 : part * 1024 + 1024] = recv[part].reshape(1024, 128).astype(F32)
    for a in range(2):
        for b in range(2):
            row = a * 256 + part * 128 + b * 64
            for c in range(4):
                target[row : row + 64, 128 * c : 128 * c + 128] = wide[
                    pl.ds(part * 1024 + c * 4 + place(a, b, epoch_first), 64, stride=16), :
                ].astype(target.dtype)


def kernel(
    x_hbm, cot_hbm, gain_s_ref, wq_s_hbm, wo_s_hbm, gain_t_ref, wq_t_hbm, wo_t_hbm,
    gin_hbm, sums_ref, gains_ref,
    x_raw, fine, wide, in_send, xs, cot_recv, ups_t, wq_s, wo_s, wq_t, wo_t,
    acted, joined_s, joined_t, probs, attended, grad_att, grad_joined, acted_t, att_t,
    mid_send, mid_recv, xt, gmid_send, gmid_recv, ups_s, gin_send, gin_recv,
    total, pair_send, pair_recv, y_send, y_recv, x1_send, x1_recv,
    xb_send, xb_recv, yb_send, yb_recv, z_send, z_recv,
    sy_send, sy_recv, sx_send, sx_recv, sz_send, sz_recv, syx_send, syx_recv, sxy_send, sxy_recv,
    szy_send, szy_recv, szx_send, szx_recv, s_send, s_recv,
    gain_send, gain_s_recv, gain_x_recv, gain_z_recv,
    send_sems, recv_sems, local_sems,
):
    dp, station, tm = lax.axis_index("dp"), lax.axis_index("station"), lax.axis_index("tm")
    y, core = station // 2, lax.rem(station, 2)
    z_hi, x_at = tm // 4, lax.rem(tm, 4)
    spot = y * 16 + tm

    def local_copy(source, target, sem):
        return pltpu.make_async_copy(source, target, local_sems.at[sem])

    def remote(source, target, sem, device):
        pltpu.make_async_remote_copy(
            src_ref=source, dst_ref=target, send_sem=send_sems.at[sem],
            recv_sem=recv_sems.at[sem], device_id=device, device_id_type=MESH,
        ).start()

    def received(ref, sem):
        pltpu.make_async_copy(ref, ref, recv_sems.at[sem]).wait()

    def sent(ref, sem):
        pltpu.make_async_copy(ref, ref, send_sems.at[sem]).wait()

    def each(first, last, action):
        def step(i, _):
            action(i)
            return 0

        lax.fori_loop(first, last, step, 0)

    loads = [
        local_copy(x_hbm, x_raw, L_X),
        local_copy(wq_s_hbm, wq_s, L_WQS),
        local_copy(wo_s_hbm, wo_s, L_WOS),
        local_copy(cot_hbm.at[pl.ds(2 * tm, 2)], cot_recv.at[:, tm], L_COT),
        local_copy(wq_t_hbm, wq_t, L_WQT),
        local_copy(wo_t_hbm, wo_t, L_WOT),
    ]
    for load in loads:
        load.start()

    barrier = pltpu.get_barrier_semaphore()

    def greet(device):
        pl.semaphore_signal(barrier, inc=1, device_id=device, device_id_type=MESH)

    each(1, 8, lambda i: greet((dp, lax.rem(station + i, 8), tm)))
    each(1, 16, lambda i: greet((dp, station, lax.rem(tm + i, 16))))
    each(0, 4, lambda i: greet((1 - dp, station, i * 4 + x_at)))
    each(1, 4, lambda i: greet((1 - dp, station, z_hi * 4 + lax.rem(x_at + i, 4))))

    loads[0].wait()
    for c in range(4):
        fine[c] = x_raw[:, :, 128 * c : 128 * c + 128].astype(F32).reshape(TOKENS, 128)
    for s in range(8):
        for e in range(2):
            for st in range(2):
                for c in range(4):
                    in_send[s, e, st, :, 128 * c : 128 * c + 128] = fine[
                        c, pl.ds(st * 16 + 2 * s + e, 16, stride=32), :
                    ].astype(BF)
    pl.semaphore_wait(barrier, 29)

    def send_in(i):
        p = lax.rem(station + i, 8)
        remote(
            in_send.at[p], xs.at[:, lax.rem(station + p, 2), :, y], R_IN, (dp, p, tm)
        )

    def send_cot(i):
        p = lax.rem(tm + i, 16)
        remote(cot_hbm.at[pl.ds(2 * p, 2)], cot_recv.at[:, tm], R_COT, (dp, station, p))

    each(1, 8, send_in)
    each(1, 16, send_cot)
    xs[:, 0, :, y] = in_send[station]

    received(in_send.at[pl.ds(0, 7)], R_IN)
    loads[1].wait()
    gain_s = gain_s_ref[...]
    _, acted_value = normalise(xs[...].reshape(TOKENS, WIDTH).astype(F32), gain_s)
    acted[0] = acted_value
    joined_s[...] = nn(acted_value, wq_s[...]).astype(BF)
    loads[2].wait()

    def send_parts(send, recv, sem, part):
        other = lax.rem(core + part, 2)

        def action(i):
            p = lax.rem(spot + i, 64)
            remote(
                send.at[part, p], recv.at[part, spot], sem + part,
                (dp, 2 * (p // 16) + other, lax.rem(p, 16)),
            )

        each(1 - part, 64, action)

    for part in range(2):
        for seq in range(2):
            for pair in range(PAIRS):
                forward_part(seq, pair, part, joined_s, probs, attended.at[0])
        x_part = jnp.concatenate(
            [xs[0, part].reshape(128, WIDTH), xs[1, part].reshape(128, WIDTH)], axis=0
        )
        mid = x_part.astype(F32) + nn(part_rows(attended.at[0], part), wo_s[...])
        pack(mid, part, True, wide, mid_send)
        send_parts(mid_send, mid_recv, R_MID, part)
    mid_recv[0, spot] = mid_send[0, spot]

    loads[3].wait()
    received(cot_recv.at[:, pl.ds(0, 15)], R_COT)
    for c in range(4):
        fine[c] = cot_recv[:, :, :, 128 * c : 128 * c + 128].astype(F32).reshape(TOKENS, 128)
    for s in range(8):
        part = lax.rem(core + s, 2)
        for st in range(2):
            for e in range(2):
                for c in range(4):
                    ups_t[st, part, e, s // 2, :, 128 * c : 128 * c + 128] = fine[
                        c, pl.ds(st * 256 + 2 * s + e, 16, stride=16), :
                    ].astype(BF)
    loads[4].wait()
    loads[5].wait()
    upstream_t = ups_t[...].reshape(TOKENS, WIDTH)
    grad_att[...] = nt(upstream_t, wo_t[...]).astype(BF)
    acted_t[0] = acted[0].T.reshape(4, 2, 64, TOKENS)
    att_t[0] = attended[0].T.reshape(4, 2, 64, TOKENS)

    gain_t = gain_t_ref[...]
    for part in range(2):
        received(mid_recv.at[part, pl.ds(0, 63 + part)], R_MID + part)
        unpack(mid_recv, part, False, wide, xt)
        _, acted_value = normalise(part_rows(xt, part), gain_t)
        put_rows(acted.at[1], part, acted_value)
        put_rows(joined_t, part, nn(acted_value, wq_t[...]).astype(BF))

    for seq in range(2):
        for pair in range(PAIRS):
            backward_step(seq, pair, joined_t, None, attended.at[1], grad_att, grad_joined)
    gain_sum_t = None
    for part in range(2):
        x_value = part_rows(xt, part)
        inverse = lax.rsqrt(jnp.mean(x_value * x_value, axis=1, keepdims=True) + EPSILON)
        grad_acted = nt(part_rows(grad_joined, part), wq_t[...])
        up_part = jnp.concatenate(
            [ups_t[0, part].reshape(128, WIDTH), ups_t[1, part].reshape(128, WIDTH)], axis=0
        )
        gain_part, grad_mid = norm_backward(
            x_value, inverse, gain_t, grad_acted, up_part.astype(F32)
        )
        gain_sum_t = gain_part if gain_sum_t is None else gain_sum_t + gain_part
        pack(grad_mid, part, False, wide, gmid_send)
        send_parts(gmid_send, gmid_recv, R_GMID, part)
    gmid_recv[0, spot] = gmid_send[0, spot]

    def products(layer, who, upstream):
        left = acted_t[layer, :, who].reshape(256, TOKENS)
        left_out = att_t[layer, :, who].reshape(256, TOKENS)
        return (
            nn(left, grad_joined[...]).reshape(4, 64, 3 * WIDTH),
            nn(left_out, upstream).reshape(4, 64, WIDTH),
        )

    def sums_send(layer, base, upstream):
        qkv, out = products(layer, 1 - core, upstream)
        pair_send[layer, :, :, 0 : 3 * WIDTH] = qkv.astype(BF)
        pair_send[layer, :, :, 3 * WIDTH :] = out.astype(BF)
        remote(pair_send.at[layer], pair_recv.at[layer], base + PAIR, (dp, 2 * y + 1 - core, tm))

    def sums_own(layer, upstream):
        qkv, out = products(layer, core, upstream)
        total[:, :, 0 : 3 * WIDTH] = qkv
        total[:, :, 3 * WIDTH :] = out

    def sums_first(layer, base):
        received(pair_recv.at[layer], base + PAIR)

        def fill(i):
            def put(t, value):
                value = value.astype(BF)
                y_send[layer, i, t] = value[0:32]
                x1_send[layer, t % 4, i, t // 4] = value[32:64]

            def piece(at):
                where = slice(at * 128, at * 128 + 128)
                return total[i, :, where] + pair_recv[layer, i, :, where].astype(F32)

            for t in range(16):
                put(t, slot(t, piece))

        each(0, 4, fill)

        def send_x(i):
            p = lax.rem(x_at + i, 4)
            remote(
                x1_send.at[layer, p], x1_recv.at[layer, x_at], base + FIRST_X,
                (dp, station, z_hi * 4 + p),
            )

        def send_y(i):
            p = lax.rem(y + i, 4)
            remote(
                y_send.at[layer, p], y_recv.at[layer, y], base + FIRST_Y, (dp, 2 * p + core, tm)
            )

        each(1, 4, send_x)
        each(1, 4, send_y)
        y_recv[layer, y] = y_send[layer, y]
        x1_recv[layer, x_at] = x1_send[layer, x_at]

    def sums_second(layer, base):
        received(x1_recv.at[layer, pl.ds(0, 3)], base + FIRST_X)

        def add_x(i):
            value = x1_recv[layer, 0, i].astype(F32)
            for j in range(1, 4):
                value = value + x1_recv[layer, j, i].astype(F32)
            yb_send[layer, i] = value.astype(BF)

        each(0, 4, add_x)

        def send_y(i):
            p = lax.rem(y + i, 4)
            remote(
                yb_send.at[layer, p], yb_recv.at[layer, y], base + SECOND_Y, (dp, 2 * p + core, tm)
            )

        each(1, 4, send_y)
        yb_recv[layer, y] = yb_send[layer, y]

        received(y_recv.at[layer, pl.ds(0, 3)], base + FIRST_Y)

        def add_y(i):
            for at in range(4):
                value = y_recv[layer, 0, 4 * i + at].astype(F32)
                for j in range(1, 4):
                    value = value + y_recv[layer, j, 4 * i + at].astype(F32)
                xb_send[layer, at, i] = value.astype(BF)

        each(0, 4, add_y)

        def send_x(i):
            p = lax.rem(x_at + i, 4)
            remote(
                xb_send.at[layer, p], xb_recv.at[layer, x_at], base + SECOND_X,
                (dp, station, z_hi * 4 + p),
            )

        each(1, 4, send_x)
        xb_recv[layer, x_at] = xb_send[layer, x_at]

    def sums_third(layer, base):
        received(yb_recv.at[layer, pl.ds(0, 3)], base + SECOND_Y)
        received(xb_recv.at[layer, pl.ds(0, 3)], base + SECOND_X)
        low, high = xb_recv[layer, 0].astype(F32), yb_recv[layer, 0].astype(F32)
        for j in range(1, 4):
            low = low + xb_recv[layer, j].astype(F32)
            high = high + yb_recv[layer, j].astype(F32)
        z_send[layer, :, 0:32] = low.astype(BF)
        z_send[layer, :, 32:64] = high.astype(BF)
        mine = 2 * z_hi + dp

        def send(i):
            p = lax.rem(mine + i, 8)
            remote(
                z_send.at[layer, p // 2], z_recv.at[layer, mine], base + THIRD,
                (lax.rem(p, 2), station, (p // 2) * 4 + x_at),
            )

        each(1, 8, send)
        z_recv[layer, mine] = z_send[layer, z_hi]

    def sums_end(layer, base):
        received(z_recv.at[layer, pl.ds(0, 7)], base + THIRD)
        value = z_recv[layer, 0].astype(F32)
        for j in range(1, 8):
            value = value + z_recv[layer, j].astype(F32)
        sums_ref[layer] = value.astype(BF)

    def along(send, recv, sem, mine, device):
        def action(i):
            p = lax.rem(mine + i, 4)
            remote(send.at[p], recv.at[mine], R_STATION + sem, device(p))

        each(1, 4, action)
        recv[mine] = send[mine]

    def at_y(p):
        return (dp, 2 * p + core, tm)

    def at_x(p):
        return (dp, station, z_hi * 4 + p)

    def at_z(p):
        return (dp, station, p * 4 + x_at)

    def gathered(recv, sem):
        received(recv.at[pl.ds(0, recv.shape[0] - 1)], R_STATION + sem)

    def summed(recv, *where):
        value = recv[(0,) + where].astype(F32)
        for j in range(1, recv.shape[0]):
            value = value + recv[(j,) + where].astype(F32)
        return value

    def station_first():
        received(pair_recv.at[0], R_STATION + PAIR)

        def fill(i):
            def piece(at):
                where = slice(at * 128, at * 128 + 128)
                return total[i, :, where] + pair_recv[0, i, :, where].astype(F32)

            for t in range(16):
                value = slot(t, piece).astype(BF)
                sy_send[i, t] = value[0:16]
                sz_send[t // 4, t % 4, i] = value[16:32]
                sx_send[t % 4, i, t // 4] = value[32:64]

        each(0, 4, fill)
        along(sz_send, sz_recv, FIRST_Z, z_hi, at_z)
        along(sx_send, sx_recv, FIRST_X, x_at, at_x)
        along(sy_send, sy_recv, FIRST_Y, y, at_y)

    def station_second():
        gathered(sy_recv, FIRST_Y)

        def add_y(i):
            for at in range(4):
                syx_send[at, i] = summed(sy_recv, 4 * i + at).astype(BF)

        each(0, 4, add_y)
        along(syx_send, syx_recv, SECOND_X, x_at, at_x)
        gathered(sz_recv, FIRST_Z)

        def add_z(i):
            for at in range(4):
                szy_send[i, at] = summed(sz_recv, at, i).astype(BF)

        each(0, 4, add_z)
        along(szy_send, szy_recv, Z_THEN_Y, y, at_y)
        gathered(sx_recv, FIRST_X)

        def add_x(i):
            sxy_send[i] = summed(sx_recv, i).astype(BF)

        each(0, 4, add_x)
        along(sxy_send, sxy_recv, SECOND_Y, y, at_y)

    def station_third():
        gathered(szy_recv, Z_THEN_Y)
        szx_send[...] = summed(szy_recv).astype(BF)
        mine_x = 2 * x_at + dp

        def send_x(i):
            p = lax.rem(mine_x + i, 8)
            remote(
                szx_send.at[p // 2], szx_recv.at[mine_x], R_STATION + Z_THEN_X,
                (lax.rem(p, 2), station, z_hi * 4 + p // 2),
            )

        each(1, 8, send_x)
        szx_recv[mine_x] = szx_send[x_at]
        gathered(syx_recv, SECOND_X)
        s_send[:, 0:16] = summed(syx_recv).astype(BF)
        gathered(sxy_recv, SECOND_Y)
        s_send[:, 16:48] = summed(sxy_recv).astype(BF)
        mine_z = 2 * z_hi + dp

        def send_z(i):
            p = lax.rem(mine_z + i, 8)
            remote(
                s_send.at[p // 2], s_recv.at[mine_z], R_STATION + THIRD,
                (lax.rem(p, 2), station, (p // 2) * 4 + x_at),
            )

        each(1, 8, send_z)
        s_recv[mine_z] = s_send[z_hi]

    def station_end():
        gathered(szx_recv, Z_THEN_X)
        sums_ref[0, 16:32] = summed(szx_recv).astype(BF)
        gathered(s_recv, THIRD)
        value = summed(s_recv).astype(BF)
        sums_ref[0, 0:16] = value[0:16]
        sums_ref[0, 32:64] = value[16:48]

    acted_t[1] = acted[1].T.reshape(4, 2, 64, TOKENS)
    att_t[1] = attended[1].T.reshape(4, 2, 64, TOKENS)
    sums_send(1, R_TIME, upstream_t)
    sums_own(1, upstream_t)
    sums_first(1, R_TIME)

    for part in range(2):
        received(gmid_recv.at[part, pl.ds(0, 63 + part)], R_GMID + part)
        unpack(gmid_recv, part, True, wide, ups_s)
        put_rows(grad_att, part, nt(part_rows(ups_s, part), wo_s[...]).astype(BF))
    for seq in range(2):
        for pair in range(PAIRS):
            backward_step(seq, pair, joined_s, probs, None, grad_att, grad_joined)
    sums_send(0, R_STATION, ups_s[...])
    sums_own(0, ups_s[...])
    grad_acted = nt(grad_joined[...], wq_s[...])
    x_value = xs[...].reshape(TOKENS, WIDTH).astype(F32)
    inverse_s = lax.rsqrt(jnp.mean(x_value * x_value, axis=1, keepdims=True) + EPSILON)
    gain_sum_s, grad_in = norm_backward(
        x_value, inverse_s, gain_s, grad_acted, ups_s[...].astype(F32)
    )
    gin_send[...] = grad_in.astype(BF).reshape(2, 2, 2, 4, 16, WIDTH)
    station_first()

    def send_gin(i):
        p = lax.rem(station + i, 8)
        remote(
            gin_send.at[:, lax.rem(station + p, 2), :, p // 2], gin_recv.at[station], R_GIN,
            (dp, p, tm),
        )

    each(1, 8, send_gin)
    gin_recv[station] = gin_send[:, 0, :, y]

    for c in range(4):
        gain_send[0, c : c + 1, :] = gain_sum_s[:, 128 * c : 128 * c + 128]
        gain_send[0, 4 + c : 5 + c, :] = gain_sum_t[:, 128 * c : 128 * c + 128]

    def send_gain_s(i):
        p = lax.rem(station + i, 8)
        remote(gain_send.at[0], gain_s_recv.at[station], R_GAIN_S, (dp, p, tm))

    each(1, 8, send_gain_s)
    gain_s_recv[station] = gain_send[0]

    sums_second(1, R_TIME)

    received(gain_s_recv.at[pl.ds(0, 7)], R_GAIN_S)
    value = gain_s_recv[0]
    for j in range(1, 8):
        value = value + gain_s_recv[j]
    gain_send[1] = value

    def send_gain_x(i):
        p = lax.rem(x_at + i, 4)
        remote(gain_send.at[1], gain_x_recv.at[x_at], R_GAIN_X, (dp, station, z_hi * 4 + p))

    each(1, 4, send_gain_x)
    gain_x_recv[x_at] = value
    station_second()
    sums_third(1, R_TIME)

    received(gain_x_recv.at[pl.ds(0, 3)], R_GAIN_X)
    value = gain_x_recv[0]
    for j in range(1, 4):
        value = value + gain_x_recv[j]
    gain_send[2] = value
    mine = 2 * z_hi + dp

    def send_gain_z(i):
        p = lax.rem(mine + i, 8)
        remote(
            gain_send.at[2], gain_z_recv.at[mine], R_GAIN_Z,
            (lax.rem(p, 2), station, (p // 2) * 4 + x_at),
        )

    each(1, 8, send_gain_z)
    gain_z_recv[mine] = value

    station_third()

    received(gin_recv.at[pl.ds(0, 7)], R_GIN)
    for s in range(8):
        for e in range(2):
            for st in range(2):
                for c in range(4):
                    fine[c, pl.ds(st * 16 + 2 * s + e, 16, stride=32), :] = gin_recv[
                        s, e, st, :, 128 * c : 128 * c + 128
                    ].astype(F32)
    for c in range(4):
        x_raw[:, :, 128 * c : 128 * c + 128] = fine[c].astype(BF).reshape(32, 16, 128)
    result = local_copy(x_raw, gin_hbm, L_OUT)
    result.start()

    sums_end(1, R_TIME)
    received(gain_z_recv.at[pl.ds(0, 7)], R_GAIN_Z)
    value = gain_z_recv[0]
    for j in range(1, 8):
        value = value + gain_z_recv[j]
    gains_ref[...] = value

    sent(in_send.at[pl.ds(0, 7)], R_IN)
    sent(cot_recv.at[:, pl.ds(0, 15)], R_COT)
    for part in range(2):
        sent(mid_send.at[part, pl.ds(0, 63 + part)], R_MID + part)
        sent(gmid_send.at[part, pl.ds(0, 63 + part)], R_GMID + part)
    sent(gin_recv.at[pl.ds(0, 7)], R_GIN)
    sent(gain_s_recv.at[pl.ds(0, 7)], R_GAIN_S)
    sent(gain_x_recv.at[pl.ds(0, 3)], R_GAIN_X)
    sent(gain_z_recv.at[pl.ds(0, 7)], R_GAIN_Z)
    sent(pair_send.at[1], R_TIME + PAIR)
    sent(y_recv.at[1, pl.ds(0, 3)], R_TIME + FIRST_Y)
    sent(x1_recv.at[1, pl.ds(0, 3)], R_TIME + FIRST_X)
    sent(xb_recv.at[1, pl.ds(0, 3)], R_TIME + SECOND_X)
    sent(yb_recv.at[1, pl.ds(0, 3)], R_TIME + SECOND_Y)
    sent(z_recv.at[1, pl.ds(0, 7)], R_TIME + THIRD)
    sent(pair_send.at[0], R_STATION + PAIR)
    for recv, sem in (
        (sy_recv, FIRST_Y), (sx_recv, FIRST_X), (sz_recv, FIRST_Z), (syx_recv, SECOND_X),
        (sxy_recv, SECOND_Y), (szy_recv, Z_THEN_Y), (szx_recv, Z_THEN_X), (s_recv, THIRD),
    ):
        sent(recv.at[pl.ds(0, recv.shape[0] - 1)], R_STATION + sem)
    station_end()
    result.wait()


def deliver(gin, sums, gains, gin_ref, gq_s_ref, go_s_ref, gg_s_ref, gq_t_ref, go_t_ref, gg_t_ref):
    gin_ref[...] = gin[...]
    for layer, qkv_ref, out_ref in ((0, gq_s_ref, go_s_ref), (1, gq_t_ref, go_t_ref)):
        value = sums[layer].astype(F32)
        qkv_ref[...] = value[:, 0:96].astype(BF)
        out_ref[...] = value.T[96:128].astype(BF)
    for c in range(4):
        gg_s_ref[:, 128 * c : 128 * c + 128] = gains[c : c + 1]
        gg_t_ref[:, 128 * c : 128 * c + 128] = gains[4 + c : 5 + c]


def local(inputs, cotangent, station_gain, station_qkv, station_out, time_gain, time_qkv, time_out):
    any_space = pl.BlockSpec(memory_space=pl.ANY)
    vmem = pl.BlockSpec(memory_space=pltpu.VMEM)
    shape = jax.ShapeDtypeStruct
    merged = pl.pallas_call(
        kernel,
        out_shape=(shape((32, 16, WIDTH), BF), shape((2, 64, 128), BF), shape((8, 128), F32)),
        in_specs=[any_space, any_space, vmem, any_space, any_space, vmem, any_space, any_space],
        out_specs=[any_space, vmem, vmem],
        scratch_shapes=[
            pltpu.VMEM((32, 16, WIDTH), BF),
            pltpu.VMEM((4, TOKENS, 128), F32),
            pltpu.VMEM((PEERS * 16, 128), F32),
            pltpu.VMEM((8, 2, 2, 16, WIDTH), BF),
            pltpu.VMEM((2, 2, 2, 4, 16, WIDTH), BF),
            pltpu.VMEM((2, 16, 16, WIDTH), BF),
            pltpu.VMEM((2, 2, 2, 4, 16, WIDTH), BF),
            pltpu.VMEM((WIDTH, 3 * WIDTH), BF),
            pltpu.VMEM((WIDTH, WIDTH), BF),
            pltpu.VMEM((WIDTH, 3 * WIDTH), BF),
            pltpu.VMEM((WIDTH, WIDTH), BF),
            pltpu.VMEM((2, TOKENS, WIDTH), BF),
            pltpu.VMEM((TOKENS, 3 * WIDTH), BF),
            pltpu.VMEM((TOKENS, 3 * WIDTH), BF),
            pltpu.VMEM((8, SEQ, 2 * SEQ), F32),
            pltpu.VMEM((2, TOKENS, WIDTH), BF),
            pltpu.VMEM((TOKENS, WIDTH), BF),
            pltpu.VMEM((TOKENS, 3 * WIDTH), BF),
            pltpu.VMEM((2, 4, 2, 64, TOKENS), BF),
            pltpu.VMEM((2, 4, 2, 64, TOKENS), BF),
            pltpu.VMEM((2, 64, 16, 128), BF),
            pltpu.VMEM((2, 64, 16, 128), BF),
            pltpu.VMEM((TOKENS, WIDTH), F32),
            pltpu.VMEM((2, 64, 16, 128), BF),
            pltpu.VMEM((2, 64, 16, 128), BF),
            pltpu.VMEM((TOKENS, WIDTH), BF),
            pltpu.VMEM((2, 2, 2, 4, 16, WIDTH), BF),
            pltpu.VMEM((8, 2, 2, 16, WIDTH), BF),
            pltpu.VMEM((4, 64, 4 * WIDTH), F32),
            pltpu.VMEM((2, 4, 64, 4 * WIDTH), BF),
            pltpu.VMEM((2, 4, 64, 4 * WIDTH), BF),
            pltpu.VMEM((2, 4, 16, 32, 128), BF),
            pltpu.VMEM((2, 4, 16, 32, 128), BF),
            pltpu.VMEM((2, 4, 4, 4, 32, 128), BF),
            pltpu.VMEM((2, 4, 4, 4, 32, 128), BF),
            pltpu.VMEM((2, 4, 4, 32, 128), BF),
            pltpu.VMEM((2, 4, 4, 32, 128), BF),
            pltpu.VMEM((2, 4, 4, 32, 128), BF),
            pltpu.VMEM((2, 4, 4, 32, 128), BF),
            pltpu.VMEM((2, 4, 64, 128), BF),
            pltpu.VMEM((2, 8, 64, 128), BF),
            pltpu.VMEM((4, 16, 16, 128), BF),
            pltpu.VMEM((4, 16, 16, 128), BF),
            pltpu.VMEM((4, 4, 4, 32, 128), BF),
            pltpu.VMEM((4, 4, 4, 32, 128), BF),
            pltpu.VMEM((4, 4, 4, 16, 128), BF),
            pltpu.VMEM((4, 4, 4, 16, 128), BF),
            pltpu.VMEM((4, 4, 16, 128), BF),
            pltpu.VMEM((4, 4, 16, 128), BF),
            pltpu.VMEM((4, 4, 32, 128), BF),
            pltpu.VMEM((4, 4, 32, 128), BF),
            pltpu.VMEM((4, 4, 16, 128), BF),
            pltpu.VMEM((4, 4, 16, 128), BF),
            pltpu.VMEM((4, 16, 128), BF),
            pltpu.VMEM((8, 16, 128), BF),
            pltpu.VMEM((4, 48, 128), BF),
            pltpu.VMEM((8, 48, 128), BF),
            pltpu.VMEM((3, 8, 128), F32),
            pltpu.VMEM((8, 8, 128), F32),
            pltpu.VMEM((4, 8, 128), F32),
            pltpu.VMEM((8, 8, 128), F32),
            pltpu.SemaphoreType.DMA((N_SEMS,)),
            pltpu.SemaphoreType.DMA((N_SEMS,)),
            pltpu.SemaphoreType.DMA((7,)),
        ],
        compiler_params=pltpu.CompilerParams(
            collective_id=0, has_side_effects=True, vmem_limit_bytes=60 * 2**20
        ),
    )(
        inputs.reshape(32, 16, WIDTH), cotangent.reshape(32, 16, WIDTH),
        station_gain.reshape(1, WIDTH), station_qkv, station_out,
        time_gain.reshape(1, WIDTH), time_qkv, time_out,
    )
    grad_in, qkv_s, out_s, gain_s, qkv_t, out_t, gain_t = pl.pallas_call(
        deliver,
        out_shape=(
            shape((32, 16, WIDTH), BF),
            shape((64, 96), BF), shape((32, 64), BF), shape((1, WIDTH), F32),
            shape((64, 96), BF), shape((32, 64), BF), shape((1, WIDTH), F32),
        ),
        in_specs=[vmem] * 3,
        out_specs=[vmem] * 7,
    )(*merged)
    return (
        grad_in.reshape(inputs.shape),
        qkv_s, out_s.T, gain_s.reshape(WIDTH), qkv_t, out_t.T, gain_t.reshape(WIDTH),
    )


def solution(mesh):
    rows = P("dp", "station", "tm", None)
    split = P("station", "tm")
    return jax.shard_map(
        local,
        mesh=mesh,
        in_specs=(rows, rows, P(), P(), P(), P(), P(), P()),
        out_specs=(rows, split, split, P(), split, split, P()),
        check_vma=False,
    )
```

```python
import functools

import jax
import jax.numpy as jnp
from jax import lax
from jax.experimental import pallas as pl
from jax.experimental.pallas import tpu as pltpu
from jax.sharding import PartitionSpec as P

MESH = pl.DeviceIdType.MESH
BF = jnp.bfloat16
F32 = jnp.float32
EPSILON = 1e-05
WIDTH = 512
TOKENS = 512
SEQ = 256
PAIRS = 4
PEERS = 128

R_IN, R_COT, R_GIN, R_GAIN_S, R_GAIN_X, R_GAIN_Z, R_MID, R_GMID, R_TIME, R_STATION = (
    0, 1, 2, 3, 4, 5, 6, 8, 10, 16,
)
PAIR, FIRST_Y, FIRST_X, SECOND_X, SECOND_Y, THIRD = range(6)
N_SEMS = 22
L_X, L_COT, L_WQS, L_WOS, L_WQT, L_WOT, L_OUT = range(7)
CHUNK = 128


def nn(a, b):
    return jnp.dot(a, b, preferred_element_type=F32)


def nt(a, b):
    return lax.dot_general(a, b, (((1,), (1,)), ((), ())), preferred_element_type=F32)


def tn(a, b):
    return lax.dot_general(a, b, (((0,), (0,)), ((), ())), preferred_element_type=F32)


def columns(pair, base=0):
    return slice(base + pair * 128, base + pair * 128 + 128)


def half_masks(value):
    lane = lax.broadcasted_iota(jnp.int32, (1, 128), 1)
    first = jnp.where(lane < 64, value, 0.0).astype(BF)
    second = jnp.where(lane < 64, 0.0, value).astype(BF)
    return first, second


def stacked(block, masks):
    return jnp.concatenate([block * masks[0], block * masks[1]], axis=0)


def under(block):
    return jnp.concatenate([block[:, :CHUNK], block[:, CHUNK:]], axis=0)


def softmax_t(scores):
    expon = jnp.exp(scores)
    total = jnp.sum(expon, axis=0, keepdims=True)
    shrink = jnp.where(total > 1.0, 0.25, 1.0)
    return (expon * shrink) * (1.0 / (total * shrink))


def forward_part(seq, pair, part, joined, probs, attended):
    rows = slice(seq * SEQ, seq * SEQ + SEQ)
    own = slice(seq * SEQ + part * CHUNK, seq * SEQ + part * CHUNK + CHUNK)
    queries = stacked(joined[own, columns(pair)], half_masks(0.125))
    values = stacked(joined[rows, columns(pair, 2 * WIDTH)], half_masks(1.0))
    p = softmax_t(nt(joined[rows, columns(pair, WIDTH)], queries))
    probs[seq * PAIRS + pair, :, part * 2 * CHUNK : part * 2 * CHUNK + 2 * CHUNK] = p
    attended[own, columns(pair)] = tn(under(p.astype(BF)), values).astype(BF)


def backward_step(seq, pair, joined, probs, attended, grad_att, grad_joined):
    rows = slice(seq * SEQ, seq * SEQ + SEQ)
    eighths = half_masks(0.125)
    ones = half_masks(1.0)
    keys = joined[rows, columns(pair, WIDTH)]
    values = joined[rows, columns(pair, 2 * WIDTH)]
    key_rows = stacked(keys, eighths)
    if probs is None:
        value_rows = stacked(values, ones)
    qs, us, p_halves, grad_ss = [], [], [], []
    for part in range(SEQ // CHUNK):
        own = slice(seq * SEQ + part * CHUNK, seq * SEQ + part * CHUNK + CHUNK)
        q = stacked(joined[own, columns(pair)], eighths)
        u = stacked(grad_att[own, columns(pair)], ones)
        if probs is None:
            p = softmax_t(nt(keys, q))
        else:
            p = probs[seq * PAIRS + pair, :, part * 2 * CHUNK : part * 2 * CHUNK + 2 * CHUNK]
        p_half = p.astype(BF)
        if probs is None:
            attended[own, columns(pair)] = tn(under(p_half), value_rows).astype(BF)
        grad_p = nt(values, u)
        dot = jnp.sum(grad_p * p, axis=0, keepdims=True)
        grad_s = (p * (grad_p - dot)).astype(BF)
        grad_joined[own, columns(pair)] = tn(under(grad_s), key_rows).astype(BF)
        qs.append(q)
        us.append(u)
        p_halves.append(p_half)
        grad_ss.append(grad_s)
    join = jnp.concatenate
    grad_joined[rows, columns(pair, WIDTH)] = nn(join(grad_ss, axis=1), join(qs, axis=0)).astype(BF)
    grad_joined[rows, columns(pair, 2 * WIDTH)] = nn(
        join(p_halves, axis=1), join(us, axis=0)
    ).astype(BF)


def normalise(x, gain):
    inverse = lax.rsqrt(jnp.mean(x * x, axis=1, keepdims=True) + EPSILON)
    normed = x * inverse
    return inverse, (normed * gain).astype(BF)


def norm_backward(x, inverse, gain, grad_acted, upstream):
    normed = x * inverse
    grad_gain = jnp.sum(grad_acted * normed, axis=0, keepdims=True)
    grad_normed = grad_acted * gain
    mean = jnp.mean(grad_normed * normed, axis=1, keepdims=True)
    return grad_gain, upstream + inverse * (grad_normed - normed * mean)


def part_rows(ref, part):
    return jnp.concatenate([ref[part * 128 : part * 128 + 128], ref[256 + part * 128 : 384 + part * 128]], axis=0)


def put_rows(ref, part, value):
    ref[part * 128 : part * 128 + 128] = value[0:128]
    ref[256 + part * 128 : 384 + part * 128] = value[128:256]


def place(a, b, epoch_first):
    return a * 2 + b if epoch_first else b * 2 + a


def pack(value, part, epoch_first, wide, send):
    for a in range(2):
        for b in range(2):
            block = value[a * 128 + b * 64 : a * 128 + b * 64 + 64]
            for c in range(4):
                wide[
                    pl.ds(part * 1024 + c * 4 + place(a, b, epoch_first), 64, stride=16), :
                ] = block[:, 128 * c : 128 * c + 128]
    send[part] = wide[part * 1024 : part * 1024 + 1024].astype(BF).reshape(64, 16, 128)


def unpack(recv, part, epoch_first, wide, target):
    wide[part * 1024 : part * 1024 + 1024] = recv[part].reshape(1024, 128).astype(F32)
    for a in range(2):
        for b in range(2):
            row = a * 256 + part * 128 + b * 64
            for c in range(4):
                target[row : row + 64, 128 * c : 128 * c + 128] = wide[
                    pl.ds(part * 1024 + c * 4 + place(a, b, epoch_first), 64, stride=16), :
                ].astype(target.dtype)


def kernel(
    x_hbm, cot_hbm, gain_s_ref, wq_s_hbm, wo_s_hbm, gain_t_ref, wq_t_hbm, wo_t_hbm,
    gin_hbm, sums_ref, gains_ref,
    x_raw, fine, wide, in_send, xs, cot_recv, ups_t, wq_s, wo_s, wq_t, wo_t,
    acted, joined_s, joined_t, probs, attended, grad_att, grad_joined, acted_t, att_t,
    mid_send, mid_recv, xt, gmid_send, gmid_recv, ups_s, gin_send, gin_recv,
    total, pair_send, pair_recv, y_send, y_recv, x1_send, x1_recv,
    xb_send, xb_recv, yb_send, yb_recv, z_send, z_recv,
    gain_send, gain_s_recv, gain_x_recv, gain_z_recv,
    send_sems, recv_sems, local_sems,
):
    dp, station, tm = lax.axis_index("dp"), lax.axis_index("station"), lax.axis_index("tm")
    y, core = station // 2, lax.rem(station, 2)
    z_hi, x_at = tm // 4, lax.rem(tm, 4)
    spot = y * 16 + tm

    def local_copy(source, target, sem):
        return pltpu.make_async_copy(source, target, local_sems.at[sem])

    def remote(source, target, sem, device):
        pltpu.make_async_remote_copy(
            src_ref=source, dst_ref=target, send_sem=send_sems.at[sem],
            recv_sem=recv_sems.at[sem], device_id=device, device_id_type=MESH,
        ).start()

    def received(ref, sem):
        pltpu.make_async_copy(ref, ref, recv_sems.at[sem]).wait()

    def sent(ref, sem):
        pltpu.make_async_copy(ref, ref, send_sems.at[sem]).wait()

    def each(first, last, action):
        def step(i, _):
            action(i)
            return 0

        lax.fori_loop(first, last, step, 0)

    loads = [
        local_copy(x_hbm, x_raw, L_X),
        local_copy(wq_s_hbm, wq_s, L_WQS),
        local_copy(wo_s_hbm, wo_s, L_WOS),
        local_copy(cot_hbm.at[pl.ds(2 * tm, 2)], cot_recv.at[:, tm], L_COT),
        local_copy(wq_t_hbm, wq_t, L_WQT),
        local_copy(wo_t_hbm, wo_t, L_WOT),
    ]
    for load in loads:
        load.start()

    barrier = pltpu.get_barrier_semaphore()

    def greet(device):
        pl.semaphore_signal(barrier, inc=1, device_id=device, device_id_type=MESH)

    each(1, 8, lambda i: greet((dp, lax.rem(station + i, 8), tm)))
    each(1, 16, lambda i: greet((dp, station, lax.rem(tm + i, 16))))
    each(0, 4, lambda i: greet((1 - dp, station, i * 4 + x_at)))

    loads[0].wait()
    for c in range(4):
        fine[c] = x_raw[:, :, 128 * c : 128 * c + 128].astype(F32).reshape(TOKENS, 128)
    for s in range(8):
        for e in range(2):
            for st in range(2):
                for c in range(4):
                    in_send[s, e, st, :, 128 * c : 128 * c + 128] = fine[
                        c, pl.ds(st * 16 + 2 * s + e, 16, stride=32), :
                    ].astype(BF)
    pl.semaphore_wait(barrier, 26)

    def send_in(i):
        p = lax.rem(station + i, 8)
        remote(
            in_send.at[p], xs.at[:, lax.rem(station + p, 2), :, y], R_IN, (dp, p, tm)
        )

    def send_cot(i):
        p = lax.rem(tm + i, 16)
        remote(cot_hbm.at[pl.ds(2 * p, 2)], cot_recv.at[:, tm], R_COT, (dp, station, p))

    each(1, 8, send_in)
    each(1, 16, send_cot)
    xs[:, 0, :, y] = in_send[station]

    received(in_send.at[pl.ds(0, 7)], R_IN)
    loads[1].wait()
    gain_s = gain_s_ref[...]
    _, acted_value = normalise(xs[...].reshape(TOKENS, WIDTH).astype(F32), gain_s)
    acted[0] = acted_value
    joined_s[...] = nn(acted_value, wq_s[...]).astype(BF)
    loads[2].wait()

    def send_parts(send, recv, sem, part):
        other = lax.rem(core + part, 2)

        def action(i):
            p = lax.rem(spot + i, 64)
            remote(
                send.at[part, p], recv.at[part, spot], sem + part,
                (dp, 2 * (p // 16) + other, lax.rem(p, 16)),
            )

        each(1 - part, 64, action)

    for part in range(2):
        for seq in range(2):
            for pair in range(PAIRS):
                forward_part(seq, pair, part, joined_s, probs, attended.at[0])
        x_part = jnp.concatenate(
            [xs[0, part].reshape(128, WIDTH), xs[1, part].reshape(128, WIDTH)], axis=0
        )
        mid = x_part.astype(F32) + nn(part_rows(attended.at[0], part), wo_s[...])
        pack(mid, part, True, wide, mid_send)
        send_parts(mid_send, mid_recv, R_MID, part)
    mid_recv[0, spot] = mid_send[0, spot]

    loads[3].wait()
    received(cot_recv.at[:, pl.ds(0, 15)], R_COT)
    for c in range(4):
        fine[c] = cot_recv[:, :, :, 128 * c : 128 * c + 128].astype(F32).reshape(TOKENS, 128)
    for s in range(8):
        part = lax.rem(core + s, 2)
        for st in range(2):
            for e in range(2):
                for c in range(4):
                    ups_t[st, part, e, s // 2, :, 128 * c : 128 * c + 128] = fine[
                        c, pl.ds(st * 256 + 2 * s + e, 16, stride=16), :
                    ].astype(BF)
    loads[4].wait()
    loads[5].wait()
    upstream_t = ups_t[...].reshape(TOKENS, WIDTH)
    grad_att[...] = nt(upstream_t, wo_t[...]).astype(BF)
    acted_t[0] = acted[0].T.reshape(4, 2, 64, TOKENS)
    att_t[0] = attended[0].T.reshape(4, 2, 64, TOKENS)

    gain_t = gain_t_ref[...]
    for part in range(2):
        received(mid_recv.at[part, pl.ds(0, 63 + part)], R_MID + part)
        unpack(mid_recv, part, False, wide, xt)
        _, acted_value = normalise(part_rows(xt, part), gain_t)
        put_rows(acted.at[1], part, acted_value)
        put_rows(joined_t, part, nn(acted_value, wq_t[...]).astype(BF))

    for seq in range(2):
        for pair in range(PAIRS):
            backward_step(seq, pair, joined_t, None, attended.at[1], grad_att, grad_joined)
    gain_sum_t = None
    for part in range(2):
        x_value = part_rows(xt, part)
        inverse = lax.rsqrt(jnp.mean(x_value * x_value, axis=1, keepdims=True) + EPSILON)
        grad_acted = nt(part_rows(grad_joined, part), wq_t[...])
        up_part = jnp.concatenate(
            [ups_t[0, part].reshape(128, WIDTH), ups_t[1, part].reshape(128, WIDTH)], axis=0
        )
        gain_part, grad_mid = norm_backward(
            x_value, inverse, gain_t, grad_acted, up_part.astype(F32)
        )
        gain_sum_t = gain_part if gain_sum_t is None else gain_sum_t + gain_part
        pack(grad_mid, part, False, wide, gmid_send)
        send_parts(gmid_send, gmid_recv, R_GMID, part)
    gmid_recv[0, spot] = gmid_send[0, spot]

    def products(layer, who, upstream):
        left = acted_t[layer, :, who].reshape(256, TOKENS)
        left_out = att_t[layer, :, who].reshape(256, TOKENS)
        return (
            nn(left, grad_joined[...]).reshape(4, 64, 3 * WIDTH),
            nn(left_out, upstream).reshape(4, 64, WIDTH),
        )

    def sums_send(layer, base, upstream):
        qkv, out = products(layer, 1 - core, upstream)
        pair_send[layer, :, :, 0 : 3 * WIDTH] = qkv.astype(BF)
        pair_send[layer, :, :, 3 * WIDTH :] = out.astype(BF)
        remote(pair_send.at[layer], pair_recv.at[layer], base + PAIR, (dp, 2 * y + 1 - core, tm))

    def sums_own(layer, upstream):
        qkv, out = products(layer, core, upstream)
        total[:, :, 0 : 3 * WIDTH] = qkv
        total[:, :, 3 * WIDTH :] = out

    def sums_first(layer, base):
        received(pair_recv.at[layer], base + PAIR)
        lane = lax.broadcasted_iota(jnp.int32, (1, 128), 1)

        def fill(i):
            def put(t, value):
                value = value.astype(BF)
                y_send[layer, i, t] = value[0:32]
                x1_send[layer, t % 4, i, t // 4] = value[32:64]

            for j in range(4):
                def piece(at):
                    where = slice(at * 128, at * 128 + 128)
                    return total[i, :, where] + pair_recv[layer, i, :, where].astype(F32)

                a, b, c, o = piece(3 * j), piece(3 * j + 1), piece(3 * j + 2), piece(12 + j)
                turn = lambda v, by: pltpu.roll(v, by, 1)
                put(4 * j, jnp.where(lane < 96, a, turn(o, 96)))
                put(4 * j + 1, jnp.where(lane < 32, turn(a, 32), jnp.where(lane < 96, turn(b, 32), turn(o, 64))))
                put(4 * j + 2, jnp.where(lane < 64, turn(b, 64), jnp.where(lane < 96, turn(c, 64), turn(o, 32))))
                put(4 * j + 3, jnp.where(lane < 96, turn(c, 96), o))

        each(0, 4, fill)

        def send_x(i):
            p = lax.rem(x_at + i, 4)
            remote(
                x1_send.at[layer, p], x1_recv.at[layer, x_at], base + FIRST_X,
                (dp, station, z_hi * 4 + p),
            )

        def send_y(i):
            p = lax.rem(y + i, 4)
            remote(
                y_send.at[layer, p], y_recv.at[layer, y], base + FIRST_Y, (dp, 2 * p + core, tm)
            )

        each(1, 4, send_x)
        each(1, 4, send_y)
        y_recv[layer, y] = y_send[layer, y]
        x1_recv[layer, x_at] = x1_send[layer, x_at]

    def sums_second(layer, base):
        received(x1_recv.at[layer, pl.ds(0, 3)], base + FIRST_X)

        def add_x(i):
            value = x1_recv[layer, 0, i].astype(F32)
            for j in range(1, 4):
                value = value + x1_recv[layer, j, i].astype(F32)
            yb_send[layer, i] = value.astype(BF)

        each(0, 4, add_x)

        def send_y(i):
            p = lax.rem(y + i, 4)
            remote(
                yb_send.at[layer, p], yb_recv.at[layer, y], base + SECOND_Y, (dp, 2 * p + core, tm)
            )

        each(1, 4, send_y)
        yb_recv[layer, y] = yb_send[layer, y]

        received(y_recv.at[layer, pl.ds(0, 3)], base + FIRST_Y)

        def add_y(i):
            for at in range(4):
                value = y_recv[layer, 0, 4 * i + at].astype(F32)
                for j in range(1, 4):
                    value = value + y_recv[layer, j, 4 * i + at].astype(F32)
                xb_send[layer, at, i] = value.astype(BF)

        each(0, 4, add_y)

        def send_x(i):
            p = lax.rem(x_at + i, 4)
            remote(
                xb_send.at[layer, p], xb_recv.at[layer, x_at], base + SECOND_X,
                (dp, station, z_hi * 4 + p),
            )

        each(1, 4, send_x)
        xb_recv[layer, x_at] = xb_send[layer, x_at]

    def sums_third(layer, base):
        received(yb_recv.at[layer, pl.ds(0, 3)], base + SECOND_Y)
        received(xb_recv.at[layer, pl.ds(0, 3)], base + SECOND_X)
        low, high = xb_recv[layer, 0].astype(F32), yb_recv[layer, 0].astype(F32)
        for j in range(1, 4):
            low = low + xb_recv[layer, j].astype(F32)
            high = high + yb_recv[layer, j].astype(F32)
        z_send[layer, :, 0:32] = low.astype(BF)
        z_send[layer, :, 32:64] = high.astype(BF)
        mine = 2 * z_hi + dp

        def send(i):
            p = lax.rem(mine + i, 8)
            remote(
                z_send.at[layer, p // 2], z_recv.at[layer, mine], base + THIRD,
                (lax.rem(p, 2), station, (p // 2) * 4 + x_at),
            )

        each(1, 8, send)
        z_recv[layer, mine] = z_send[layer, z_hi]

    def sums_end(layer, base):
        received(z_recv.at[layer, pl.ds(0, 7)], base + THIRD)
        value = z_recv[layer, 0].astype(F32)
        for j in range(1, 8):
            value = value + z_recv[layer, j].astype(F32)
        sums_ref[layer] = value.astype(BF)

    acted_t[1] = acted[1].T.reshape(4, 2, 64, TOKENS)
    att_t[1] = attended[1].T.reshape(4, 2, 64, TOKENS)
    sums_send(1, R_TIME, upstream_t)
    sums_own(1, upstream_t)
    sums_first(1, R_TIME)

    for part in range(2):
        received(gmid_recv.at[part, pl.ds(0, 63 + part)], R_GMID + part)
        unpack(gmid_recv, part, True, wide, ups_s)
        put_rows(grad_att, part, nt(part_rows(ups_s, part), wo_s[...]).astype(BF))
    for seq in range(2):
        for pair in range(PAIRS):
            backward_step(seq, pair, joined_s, probs, None, grad_att, grad_joined)
    sums_send(0, R_STATION, ups_s[...])
    sums_second(1, R_TIME)
    grad_acted = nt(grad_joined[...], wq_s[...])
    x_value = xs[...].reshape(TOKENS, WIDTH).astype(F32)
    inverse_s = lax.rsqrt(jnp.mean(x_value * x_value, axis=1, keepdims=True) + EPSILON)
    gain_sum_s, grad_in = norm_backward(
        x_value, inverse_s, gain_s, grad_acted, ups_s[...].astype(F32)
    )
    gin_send[...] = grad_in.astype(BF).reshape(2, 2, 2, 4, 16, WIDTH)

    def send_gin(i):
        p = lax.rem(station + i, 8)
        remote(
            gin_send.at[:, lax.rem(station + p, 2), :, p // 2], gin_recv.at[station], R_GIN,
            (dp, p, tm),
        )

    each(1, 8, send_gin)
    gin_recv[station] = gin_send[:, 0, :, y]

    for c in range(4):
        gain_send[0, c : c + 1, :] = gain_sum_s[:, 128 * c : 128 * c + 128]
        gain_send[0, 4 + c : 5 + c, :] = gain_sum_t[:, 128 * c : 128 * c + 128]

    def send_gain_s(i):
        p = lax.rem(station + i, 8)
        remote(gain_send.at[0], gain_s_recv.at[station], R_GAIN_S, (dp, p, tm))

    each(1, 8, send_gain_s)
    gain_s_recv[station] = gain_send[0]

    sums_own(0, ups_s[...])
    sums_first(0, R_STATION)
    sums_third(1, R_TIME)

    received(gain_s_recv.at[pl.ds(0, 7)], R_GAIN_S)
    value = gain_s_recv[0]
    for j in range(1, 8):
        value = value + gain_s_recv[j]
    gain_send[1] = value

    def send_gain_x(i):
        p = lax.rem(x_at + i, 4)
        remote(gain_send.at[1], gain_x_recv.at[x_at], R_GAIN_X, (dp, station, z_hi * 4 + p))

    each(1, 4, send_gain_x)
    gain_x_recv[x_at] = value
    sums_end(1, R_TIME)

    received(gain_x_recv.at[pl.ds(0, 3)], R_GAIN_X)
    value = gain_x_recv[0]
    for j in range(1, 4):
        value = value + gain_x_recv[j]
    gain_send[2] = value
    mine = 2 * z_hi + dp

    def send_gain_z(i):
        p = lax.rem(mine + i, 8)
        remote(
            gain_send.at[2], gain_z_recv.at[mine], R_GAIN_Z,
            (lax.rem(p, 2), station, (p // 2) * 4 + x_at),
        )

    each(1, 8, send_gain_z)
    gain_z_recv[mine] = value

    sums_second(0, R_STATION)

    received(gin_recv.at[pl.ds(0, 7)], R_GIN)
    for s in range(8):
        for e in range(2):
            for st in range(2):
                for c in range(4):
                    fine[c, pl.ds(st * 16 + 2 * s + e, 16, stride=32), :] = gin_recv[
                        s, e, st, :, 128 * c : 128 * c + 128
                    ].astype(F32)
    for c in range(4):
        x_raw[:, :, 128 * c : 128 * c + 128] = fine[c].astype(BF).reshape(32, 16, 128)
    result = local_copy(x_raw, gin_hbm, L_OUT)
    result.start()

    sums_third(0, R_STATION)
    received(gain_z_recv.at[pl.ds(0, 7)], R_GAIN_Z)
    value = gain_z_recv[0]
    for j in range(1, 8):
        value = value + gain_z_recv[j]
    gains_ref[...] = value

    sent(in_send.at[pl.ds(0, 7)], R_IN)
    sent(cot_recv.at[:, pl.ds(0, 15)], R_COT)
    for part in range(2):
        sent(mid_send.at[part, pl.ds(0, 63 + part)], R_MID + part)
        sent(gmid_send.at[part, pl.ds(0, 63 + part)], R_GMID + part)
    sent(gin_recv.at[pl.ds(0, 7)], R_GIN)
    sent(gain_s_recv.at[pl.ds(0, 7)], R_GAIN_S)
    sent(gain_x_recv.at[pl.ds(0, 3)], R_GAIN_X)
    sent(gain_z_recv.at[pl.ds(0, 7)], R_GAIN_Z)
    for layer, base in ((1, R_TIME), (0, R_STATION)):
        sent(pair_send.at[layer], base + PAIR)
        sent(y_recv.at[layer, pl.ds(0, 3)], base + FIRST_Y)
        sent(x1_recv.at[layer, pl.ds(0, 3)], base + FIRST_X)
        sent(xb_recv.at[layer, pl.ds(0, 3)], base + SECOND_X)
        sent(yb_recv.at[layer, pl.ds(0, 3)], base + SECOND_Y)
        sent(z_recv.at[layer, pl.ds(0, 7)], base + THIRD)
    sums_end(0, R_STATION)
    result.wait()


def deliver(gin, sums, gains, gin_ref, gq_s_ref, go_s_ref, gg_s_ref, gq_t_ref, go_t_ref, gg_t_ref):
    gin_ref[...] = gin[...]
    for layer, qkv_ref, out_ref in ((0, gq_s_ref, go_s_ref), (1, gq_t_ref, go_t_ref)):
        value = sums[layer].astype(F32)
        qkv_ref[...] = value[:, 0:96].astype(BF)
        out_ref[...] = value.T[96:128].astype(BF)
    for c in range(4):
        gg_s_ref[:, 128 * c : 128 * c + 128] = gains[c : c + 1]
        gg_t_ref[:, 128 * c : 128 * c + 128] = gains[4 + c : 5 + c]


def local(inputs, cotangent, station_gain, station_qkv, station_out, time_gain, time_qkv, time_out):
    any_space = pl.BlockSpec(memory_space=pl.ANY)
    vmem = pl.BlockSpec(memory_space=pltpu.VMEM)
    shape = jax.ShapeDtypeStruct
    merged = pl.pallas_call(
        kernel,
        out_shape=(shape((32, 16, WIDTH), BF), shape((2, 64, 128), BF), shape((8, 128), F32)),
        in_specs=[any_space, any_space, vmem, any_space, any_space, vmem, any_space, any_space],
        out_specs=[any_space, vmem, vmem],
        scratch_shapes=[
            pltpu.VMEM((32, 16, WIDTH), BF),
            pltpu.VMEM((4, TOKENS, 128), F32),
            pltpu.VMEM((PEERS * 16, 128), F32),
            pltpu.VMEM((8, 2, 2, 16, WIDTH), BF),
            pltpu.VMEM((2, 2, 2, 4, 16, WIDTH), BF),
            pltpu.VMEM((2, 16, 16, WIDTH), BF),
            pltpu.VMEM((2, 2, 2, 4, 16, WIDTH), BF),
            pltpu.VMEM((WIDTH, 3 * WIDTH), BF),
            pltpu.VMEM((WIDTH, WIDTH), BF),
            pltpu.VMEM((WIDTH, 3 * WIDTH), BF),
            pltpu.VMEM((WIDTH, WIDTH), BF),
            pltpu.VMEM((2, TOKENS, WIDTH), BF),
            pltpu.VMEM((TOKENS, 3 * WIDTH), BF),
            pltpu.VMEM((TOKENS, 3 * WIDTH), BF),
            pltpu.VMEM((8, SEQ, 2 * SEQ), F32),
            pltpu.VMEM((2, TOKENS, WIDTH), BF),
            pltpu.VMEM((TOKENS, WIDTH), BF),
            pltpu.VMEM((TOKENS, 3 * WIDTH), BF),
            pltpu.VMEM((2, 4, 2, 64, TOKENS), BF),
            pltpu.VMEM((2, 4, 2, 64, TOKENS), BF),
            pltpu.VMEM((2, 64, 16, 128), BF),
            pltpu.VMEM((2, 64, 16, 128), BF),
            pltpu.VMEM((TOKENS, WIDTH), F32),
            pltpu.VMEM((2, 64, 16, 128), BF),
            pltpu.VMEM((2, 64, 16, 128), BF),
            pltpu.VMEM((TOKENS, WIDTH), BF),
            pltpu.VMEM((2, 2, 2, 4, 16, WIDTH), BF),
            pltpu.VMEM((8, 2, 2, 16, WIDTH), BF),
            pltpu.VMEM((4, 64, 4 * WIDTH), F32),
            pltpu.VMEM((2, 4, 64, 4 * WIDTH), BF),
            pltpu.VMEM((2, 4, 64, 4 * WIDTH), BF),
            pltpu.VMEM((2, 4, 16, 32, 128), BF),
            pltpu.VMEM((2, 4, 16, 32, 128), BF),
            pltpu.VMEM((2, 4, 4, 4, 32, 128), BF),
            pltpu.VMEM((2, 4, 4, 4, 32, 128), BF),
            pltpu.VMEM((2, 4, 4, 32, 128), BF),
            pltpu.VMEM((2, 4, 4, 32, 128), BF),
            pltpu.VMEM((2, 4, 4, 32, 128), BF),
            pltpu.VMEM((2, 4, 4, 32, 128), BF),
            pltpu.VMEM((2, 4, 64, 128), BF),
            pltpu.VMEM((2, 8, 64, 128), BF),
            pltpu.VMEM((3, 8, 128), F32),
            pltpu.VMEM((8, 8, 128), F32),
            pltpu.VMEM((4, 8, 128), F32),
            pltpu.VMEM((8, 8, 128), F32),
            pltpu.SemaphoreType.DMA((N_SEMS,)),
            pltpu.SemaphoreType.DMA((N_SEMS,)),
            pltpu.SemaphoreType.DMA((7,)),
        ],
        compiler_params=pltpu.CompilerParams(
            collective_id=0, has_side_effects=True, vmem_limit_bytes=60 * 2**20
        ),
    )(
        inputs.reshape(32, 16, WIDTH), cotangent.reshape(32, 16, WIDTH),
        station_gain.reshape(1, WIDTH), station_qkv, station_out,
        time_gain.reshape(1, WIDTH), time_qkv, time_out,
    )
    grad_in, qkv_s, out_s, gain_s, qkv_t, out_t, gain_t = pl.pallas_call(
        deliver,
        out_shape=(
            shape((32, 16, WIDTH), BF),
            shape((64, 96), BF), shape((32, 64), BF), shape((1, WIDTH), F32),
            shape((64, 96), BF), shape((32, 64), BF), shape((1, WIDTH), F32),
        ),
        in_specs=[vmem] * 3,
        out_specs=[vmem] * 7,
    )(*merged)
    return (
        grad_in.reshape(inputs.shape),
        qkv_s, out_s.T, gain_s.reshape(WIDTH), qkv_t, out_t.T, gain_t.reshape(WIDTH),
    )


def solution(mesh):
    rows = P("dp", "station", "tm", None)
    split = P("station", "tm")
    return jax.shard_map(
        local,
        mesh=mesh,
        in_specs=(rows, rows, P(), P(), P(), P(), P(), P()),
        out_specs=(rows, split, split, P(), split, split, P()),
        check_vma=False,
    )
```

```python
import functools

import jax
import jax.numpy as jnp
from jax import lax
from jax.experimental import pallas as pl
from jax.experimental.pallas import tpu as pltpu
from jax.sharding import PartitionSpec as P

MESH = pl.DeviceIdType.MESH
BF = jnp.bfloat16
F32 = jnp.float32
EPSILON = 1e-05
WIDTH = 512
TOKENS = 512
SEQ = 256
PAIRS = 4
PEERS = 128

R_IN, R_COT, R_GIN, R_GAIN_S, R_GAIN_X, R_GAIN_Z, R_MID, R_GMID, R_TIME, R_STATION = (
    0, 1, 2, 3, 4, 5, 6, 8, 10, 16,
)
PAIR, FIRST_Y, FIRST_X, SECOND_X, SECOND_Y, THIRD = range(6)
R_INS = (R_IN, 22)
R_COTS = (R_COT, 23)
N_SEMS = 24
L_X, L_COT, L_WQS, L_WOS, L_WQT, L_WOT, L_OUT = range(7)
CHUNK = 128


def nn(a, b):
    return jnp.dot(a, b, preferred_element_type=F32)


def nt(a, b):
    return lax.dot_general(a, b, (((1,), (1,)), ((), ())), preferred_element_type=F32)


def tn(a, b):
    return lax.dot_general(a, b, (((0,), (0,)), ((), ())), preferred_element_type=F32)


def columns(pair, base=0):
    return slice(base + pair * 128, base + pair * 128 + 128)


def half_masks(value):
    lane = lax.broadcasted_iota(jnp.int32, (1, 128), 1)
    first = jnp.where(lane < 64, value, 0.0).astype(BF)
    second = jnp.where(lane < 64, 0.0, value).astype(BF)
    return first, second


def stacked(block, masks):
    return jnp.concatenate([block * masks[0], block * masks[1]], axis=0)


def under(block):
    return jnp.concatenate([block[:, :CHUNK], block[:, CHUNK:]], axis=0)


def softmax_t(scores):
    expon = jnp.exp(scores)
    total = jnp.sum(expon, axis=0, keepdims=True)
    shrink = jnp.where(total > 1.0, 0.25, 1.0)
    return (expon * shrink) * (1.0 / (total * shrink))


def forward_part(seq, pair, part, joined, probs, attended):
    rows = slice(seq * SEQ, seq * SEQ + SEQ)
    own = slice(seq * SEQ + part * CHUNK, seq * SEQ + part * CHUNK + CHUNK)
    queries = stacked(joined[own, columns(pair)], half_masks(0.125))
    values = stacked(joined[rows, columns(pair, 2 * WIDTH)], half_masks(1.0))
    p = softmax_t(nt(joined[rows, columns(pair, WIDTH)], queries))
    probs[seq * PAIRS + pair, :, part * 2 * CHUNK : part * 2 * CHUNK + 2 * CHUNK] = p
    attended[own, columns(pair)] = tn(under(p.astype(BF)), values).astype(BF)


def backward_step(seq, pair, joined, probs, attended, grad_att, grad_joined):
    rows = slice(seq * SEQ, seq * SEQ + SEQ)
    eighths = half_masks(0.125)
    ones = half_masks(1.0)
    keys = joined[rows, columns(pair, WIDTH)]
    values = joined[rows, columns(pair, 2 * WIDTH)]
    key_rows = stacked(keys, eighths)
    if probs is None:
        value_rows = stacked(values, ones)
    qs, us, p_halves, grad_ss = [], [], [], []
    for part in range(SEQ // CHUNK):
        own = slice(seq * SEQ + part * CHUNK, seq * SEQ + part * CHUNK + CHUNK)
        q = stacked(joined[own, columns(pair)], eighths)
        u = stacked(grad_att[own, columns(pair)], ones)
        if probs is None:
            p = softmax_t(nt(keys, q))
        else:
            p = probs[seq * PAIRS + pair, :, part * 2 * CHUNK : part * 2 * CHUNK + 2 * CHUNK]
        p_half = p.astype(BF)
        if probs is None:
            attended[own, columns(pair)] = tn(under(p_half), value_rows).astype(BF)
        grad_p = nt(values, u)
        dot = jnp.sum(grad_p * p, axis=0, keepdims=True)
        grad_s = (p * (grad_p - dot)).astype(BF)
        grad_joined[own, columns(pair)] = tn(under(grad_s), key_rows).astype(BF)
        qs.append(q)
        us.append(u)
        p_halves.append(p_half)
        grad_ss.append(grad_s)
    join = jnp.concatenate
    grad_joined[rows, columns(pair, WIDTH)] = nn(join(grad_ss, axis=1), join(qs, axis=0)).astype(BF)
    grad_joined[rows, columns(pair, 2 * WIDTH)] = nn(
        join(p_halves, axis=1), join(us, axis=0)
    ).astype(BF)


def normalise(x, gain):
    inverse = lax.rsqrt(jnp.mean(x * x, axis=1, keepdims=True) + EPSILON)
    normed = x * inverse
    return inverse, (normed * gain).astype(BF)


def norm_backward(x, inverse, gain, grad_acted, upstream):
    normed = x * inverse
    grad_gain = jnp.sum(grad_acted * normed, axis=0, keepdims=True)
    grad_normed = grad_acted * gain
    mean = jnp.mean(grad_normed * normed, axis=1, keepdims=True)
    return grad_gain, upstream + inverse * (grad_normed - normed * mean)


def part_rows(ref, part):
    return jnp.concatenate([ref[part * 128 : part * 128 + 128], ref[256 + part * 128 : 384 + part * 128]], axis=0)


def put_rows(ref, part, value):
    ref[part * 128 : part * 128 + 128] = value[0:128]
    ref[256 + part * 128 : 384 + part * 128] = value[128:256]


def place(a, b, epoch_first):
    return a * 2 + b if epoch_first else b * 2 + a


def pack(value, part, epoch_first, wide, send):
    for a in range(2):
        for b in range(2):
            block = value[a * 128 + b * 64 : a * 128 + b * 64 + 64]
            for c in range(4):
                wide[
                    pl.ds(part * 1024 + c * 4 + place(a, b, epoch_first), 64, stride=16), :
                ] = block[:, 128 * c : 128 * c + 128]
    send[part] = wide[part * 1024 : part * 1024 + 1024].astype(BF).reshape(64, 16, 128)


def unpack(recv, part, epoch_first, wide, target):
    wide[part * 1024 : part * 1024 + 1024] = recv[part].reshape(1024, 128).astype(F32)
    for a in range(2):
        for b in range(2):
            row = a * 256 + part * 128 + b * 64
            for c in range(4):
                target[row : row + 64, 128 * c : 128 * c + 128] = wide[
                    pl.ds(part * 1024 + c * 4 + place(a, b, epoch_first), 64, stride=16), :
                ].astype(target.dtype)


def kernel(
    x_hbm, cot_hbm, gain_s_ref, wq_s_hbm, wo_s_hbm, gain_t_ref, wq_t_hbm, wo_t_hbm,
    gin_hbm, sums_ref, gains_ref,
    x_raw, fine, wide, in_send, xs, cot_recv, ups_t, wq_s, wo_s, wq_t, wo_t,
    acted, joined_s, joined_t, probs, attended, grad_att, grad_joined, acted_t, att_t,
    mid_send, mid_recv, xt, gmid_send, gmid_recv, ups_s, gin_send, gin_recv,
    total, pair_send, pair_recv, y_send, y_recv, x1_send, x1_recv,
    xb_send, xb_recv, yb_send, yb_recv, z_send, z_recv,
    gain_send, gain_s_recv, gain_x_recv, gain_z_recv,
    send_sems, recv_sems, local_sems,
):
    dp, station, tm = lax.axis_index("dp"), lax.axis_index("station"), lax.axis_index("tm")
    y, core = station // 2, lax.rem(station, 2)
    z_hi, x_at = tm // 4, lax.rem(tm, 4)
    spot = y * 16 + tm

    def local_copy(source, target, sem):
        return pltpu.make_async_copy(source, target, local_sems.at[sem])

    def remote(source, target, sem, device):
        pltpu.make_async_remote_copy(
            src_ref=source, dst_ref=target, send_sem=send_sems.at[sem],
            recv_sem=recv_sems.at[sem], device_id=device, device_id_type=MESH,
        ).start()

    def received(ref, sem):
        pltpu.make_async_copy(ref, ref, recv_sems.at[sem]).wait()

    def sent(ref, sem):
        pltpu.make_async_copy(ref, ref, send_sems.at[sem]).wait()

    def each(first, last, action):
        def step(i, _):
            action(i)
            return 0

        lax.fori_loop(first, last, step, 0)

    loads = [
        local_copy(x_hbm, x_raw, L_X),
        local_copy(wq_s_hbm, wq_s, L_WQS),
        local_copy(wo_s_hbm, wo_s, L_WOS),
        local_copy(cot_hbm.at[pl.ds(2 * tm, 2)], cot_recv.at[:, tm], L_COT),
        local_copy(wq_t_hbm, wq_t, L_WQT),
        local_copy(wo_t_hbm, wo_t, L_WOT),
    ]
    for load in loads:
        load.start()

    barrier = pltpu.get_barrier_semaphore()

    def greet(device):
        pl.semaphore_signal(barrier, inc=1, device_id=device, device_id_type=MESH)

    each(1, 8, lambda i: greet((dp, lax.rem(station + i, 8), tm)))
    each(1, 16, lambda i: greet((dp, station, lax.rem(tm + i, 16))))
    each(0, 4, lambda i: greet((1 - dp, station, i * 4 + x_at)))

    loads[0].wait()
    for c in range(4):
        fine[c] = x_raw[:, :, 128 * c : 128 * c + 128].astype(F32).reshape(TOKENS, 128)
    for s in range(8):
        for e in range(2):
            for st in range(2):
                for c in range(4):
                    in_send[s, e, st, :, 128 * c : 128 * c + 128] = fine[
                        c, pl.ds(st * 16 + 2 * s + e, 16, stride=32), :
                    ].astype(BF)
    pl.semaphore_wait(barrier, 26)

    def send_in(e):
        def action(i):
            p = lax.rem(station + i, 8)
            remote(
                in_send.at[p, e], xs.at[e, lax.rem(station + p, 2), :, y], R_INS[e], (dp, p, tm)
            )

        each(1, 8, action)

    def send_cot(st):
        def action(i):
            p = lax.rem(tm + i, 16)
            remote(cot_hbm.at[2 * p + st], cot_recv.at[st, tm], R_COTS[st], (dp, station, p))

        each(1, 16, action)

    send_in(0)
    send_in(1)
    send_cot(0)
    xs[:, 0, :, y] = in_send[station]

    loads[1].wait()
    loads[2].wait()
    gain_s = gain_s_ref[...]
    for seq in range(2):
        received(in_send.at[pl.ds(0, 7), seq], R_INS[seq])
        rows = slice(seq * SEQ, seq * SEQ + SEQ)
        _, acted_value = normalise(xs[seq].reshape(SEQ, WIDTH).astype(F32), gain_s)
        acted[0, rows] = acted_value
        joined_s[rows] = nn(acted_value, wq_s[...]).astype(BF)
        if seq == 0:
            for part in range(2):
                for pair in range(PAIRS):
                    forward_part(0, pair, part, joined_s, probs, attended.at[0])

    def send_parts(send, recv, sem, part):
        other = lax.rem(core + part, 2)

        def action(i):
            p = lax.rem(spot + i, 64)
            remote(
                send.at[part, p], recv.at[part, spot], sem + part,
                (dp, 2 * (p // 16) + other, lax.rem(p, 16)),
            )

        each(1 - part, 64, action)

    for part in range(2):
        for pair in range(PAIRS):
            forward_part(1, pair, part, joined_s, probs, attended.at[0])
        x_part = jnp.concatenate(
            [xs[0, part].reshape(128, WIDTH), xs[1, part].reshape(128, WIDTH)], axis=0
        )
        mid = x_part.astype(F32) + nn(part_rows(attended.at[0], part), wo_s[...])
        pack(mid, part, True, wide, mid_send)
        send_parts(mid_send, mid_recv, R_MID, part)
    mid_recv[0, spot] = mid_send[0, spot]

    send_cot(1)

    def take_cot(st):
        received(cot_recv.at[st, pl.ds(0, 15)], R_COTS[st])
        for c in range(4):
            fine[c, 0:SEQ] = cot_recv[st, :, :, 128 * c : 128 * c + 128].astype(F32).reshape(SEQ, 128)
        for s in range(8):
            part = lax.rem(core + s, 2)
            for e in range(2):
                for c in range(4):
                    ups_t[st, part, e, s // 2, :, 128 * c : 128 * c + 128] = fine[
                        c, pl.ds(2 * s + e, 16, stride=16), :
                    ].astype(BF)
        grad_att[st * SEQ : st * SEQ + SEQ] = nt(
            ups_t[st].reshape(SEQ, WIDTH), wo_t[...]
        ).astype(BF)

    for k in range(3, 6):
        loads[k].wait()
    take_cot(0)
    acted_t[0] = acted[0].T.reshape(4, 2, 64, TOKENS)
    att_t[0] = attended[0].T.reshape(4, 2, 64, TOKENS)

    gain_t = gain_t_ref[...]
    for part in range(2):
        received(mid_recv.at[part, pl.ds(0, 63 + part)], R_MID + part)
        unpack(mid_recv, part, False, wide, xt)
        _, acted_value = normalise(part_rows(xt, part), gain_t)
        put_rows(acted.at[1], part, acted_value)
        put_rows(joined_t, part, nn(acted_value, wq_t[...]).astype(BF))

    for seq in range(2):
        if seq == 1:
            take_cot(1)
        for pair in range(PAIRS):
            backward_step(seq, pair, joined_t, None, attended.at[1], grad_att, grad_joined)
    upstream_t = ups_t[...].reshape(TOKENS, WIDTH)
    gain_sum_t = None
    for part in range(2):
        x_value = part_rows(xt, part)
        inverse = lax.rsqrt(jnp.mean(x_value * x_value, axis=1, keepdims=True) + EPSILON)
        grad_acted = nt(part_rows(grad_joined, part), wq_t[...])
        up_part = jnp.concatenate(
            [ups_t[0, part].reshape(128, WIDTH), ups_t[1, part].reshape(128, WIDTH)], axis=0
        )
        gain_part, grad_mid = norm_backward(
            x_value, inverse, gain_t, grad_acted, up_part.astype(F32)
        )
        gain_sum_t = gain_part if gain_sum_t is None else gain_sum_t + gain_part
        pack(grad_mid, part, False, wide, gmid_send)
        send_parts(gmid_send, gmid_recv, R_GMID, part)
    gmid_recv[0, spot] = gmid_send[0, spot]

    def products(layer, who, upstream):
        left = acted_t[layer, :, who].reshape(256, TOKENS)
        left_out = att_t[layer, :, who].reshape(256, TOKENS)
        return (
            nn(left, grad_joined[...]).reshape(4, 64, 3 * WIDTH),
            nn(left_out, upstream).reshape(4, 64, WIDTH),
        )

    def sums_send(layer, base, upstream):
        qkv, out = products(layer, 1 - core, upstream)
        pair_send[layer, :, :, 0 : 3 * WIDTH] = qkv.astype(BF)
        pair_send[layer, :, :, 3 * WIDTH :] = out.astype(BF)
        remote(pair_send.at[layer], pair_recv.at[layer], base + PAIR, (dp, 2 * y + 1 - core, tm))

    def sums_own(layer, upstream):
        qkv, out = products(layer, core, upstream)
        total[:, :, 0 : 3 * WIDTH] = qkv
        total[:, :, 3 * WIDTH :] = out

    def sums_first(layer, base):
        received(pair_recv.at[layer], base + PAIR)
        lane = lax.broadcasted_iota(jnp.int32, (1, 128), 1)

        def fill(i):
            def put(t, value):
                value = value.astype(BF)
                y_send[layer, i, t] = value[0:32]
                x1_send[layer, t % 4, i, t // 4] = value[32:64]

            for j in range(4):
                def piece(at):
                    where = slice(at * 128, at * 128 + 128)
                    return total[i, :, where] + pair_recv[layer, i, :, where].astype(F32)

                a, b, c, o = piece(3 * j), piece(3 * j + 1), piece(3 * j + 2), piece(12 + j)
                turn = lambda v, by: pltpu.roll(v, by, 1)
                put(4 * j, jnp.where(lane < 96, a, turn(o, 96)))
                put(4 * j + 1, jnp.where(lane < 32, turn(a, 32), jnp.where(lane < 96, turn(b, 32), turn(o, 64))))
                put(4 * j + 2, jnp.where(lane < 64, turn(b, 64), jnp.where(lane < 96, turn(c, 64), turn(o, 32))))
                put(4 * j + 3, jnp.where(lane < 96, turn(c, 96), o))

        each(0, 4, fill)

        def send_x(i):
            p = lax.rem(x_at + i, 4)
            remote(
                x1_send.at[layer, p], x1_recv.at[layer, x_at], base + FIRST_X,
                (dp, station, z_hi * 4 + p),
            )

        def send_y(i):
            p = lax.rem(y + i, 4)
            remote(
                y_send.at[layer, p], y_recv.at[layer, y], base + FIRST_Y, (dp, 2 * p + core, tm)
            )

        each(1, 4, send_x)
        each(1, 4, send_y)
        y_recv[layer, y] = y_send[layer, y]
        x1_recv[layer, x_at] = x1_send[layer, x_at]

    def sums_second(layer, base):
        received(x1_recv.at[layer, pl.ds(0, 3)], base + FIRST_X)

        def add_x(i):
            value = x1_recv[layer, 0, i].astype(F32)
            for j in range(1, 4):
                value = value + x1_recv[layer, j, i].astype(F32)
            yb_send[layer, i] = value.astype(BF)

        each(0, 4, add_x)

        def send_y(i):
            p = lax.rem(y + i, 4)
            remote(
                yb_send.at[layer, p], yb_recv.at[layer, y], base + SECOND_Y, (dp, 2 * p + core, tm)
            )

        each(1, 4, send_y)
        yb_recv[layer, y] = yb_send[layer, y]

        received(y_recv.at[layer, pl.ds(0, 3)], base + FIRST_Y)

        def add_y(i):
            for at in range(4):
                value = y_recv[layer, 0, 4 * i + at].astype(F32)
                for j in range(1, 4):
                    value = value + y_recv[layer, j, 4 * i + at].astype(F32)
                xb_send[layer, at, i] = value.astype(BF)

        each(0, 4, add_y)

        def send_x(i):
            p = lax.rem(x_at + i, 4)
            remote(
                xb_send.at[layer, p], xb_recv.at[layer, x_at], base + SECOND_X,
                (dp, station, z_hi * 4 + p),
            )

        each(1, 4, send_x)
        xb_recv[layer, x_at] = xb_send[layer, x_at]

    def sums_third(layer, base):
        received(yb_recv.at[layer, pl.ds(0, 3)], base + SECOND_Y)
        received(xb_recv.at[layer, pl.ds(0, 3)], base + SECOND_X)
        low, high = xb_recv[layer, 0].astype(F32), yb_recv[layer, 0].astype(F32)
        for j in range(1, 4):
            low = low + xb_recv[layer, j].astype(F32)
            high = high + yb_recv[layer, j].astype(F32)
        z_send[layer, :, 0:32] = low.astype(BF)
        z_send[layer, :, 32:64] = high.astype(BF)
        mine = 2 * z_hi + dp

        def send(i):
            p = lax.rem(mine + i, 8)
            remote(
                z_send.at[layer, p // 2], z_recv.at[layer, mine], base + THIRD,
                (lax.rem(p, 2), station, (p // 2) * 4 + x_at),
            )

        each(1, 8, send)
        z_recv[layer, mine] = z_send[layer, z_hi]

    def sums_end(layer, base):
        received(z_recv.at[layer, pl.ds(0, 7)], base + THIRD)
        value = z_recv[layer, 0].astype(F32)
        for j in range(1, 8):
            value = value + z_recv[layer, j].astype(F32)
        sums_ref[layer] = value.astype(BF)

    acted_t[1] = acted[1].T.reshape(4, 2, 64, TOKENS)
    att_t[1] = attended[1].T.reshape(4, 2, 64, TOKENS)
    sums_send(1, R_TIME, upstream_t)
    sums_own(1, upstream_t)
    sums_first(1, R_TIME)

    for part in range(2):
        received(gmid_recv.at[part, pl.ds(0, 63 + part)], R_GMID + part)
        unpack(gmid_recv, part, True, wide, ups_s)
        put_rows(grad_att, part, nt(part_rows(ups_s, part), wo_s[...]).astype(BF))
    for seq in range(2):
        for pair in range(PAIRS):
            backward_step(seq, pair, joined_s, probs, None, grad_att, grad_joined)
    sums_send(0, R_STATION, ups_s[...])
    sums_second(1, R_TIME)
    grad_acted = nt(grad_joined[...], wq_s[...])
    x_value = xs[...].reshape(TOKENS, WIDTH).astype(F32)
    inverse_s = lax.rsqrt(jnp.mean(x_value * x_value, axis=1, keepdims=True) + EPSILON)
    gain_sum_s, grad_in = norm_backward(
        x_value, inverse_s, gain_s, grad_acted, ups_s[...].astype(F32)
    )
    gin_send[...] = grad_in.astype(BF).reshape(2, 2, 2, 4, 16, WIDTH)

    def send_gin(i):
        p = lax.rem(station + i, 8)
        remote(
            gin_send.at[:, lax.rem(station + p, 2), :, p // 2], gin_recv.at[station], R_GIN,
            (dp, p, tm),
        )

    each(1, 8, send_gin)
    gin_recv[station] = gin_send[:, 0, :, y]

    for c in range(4):
        gain_send[0, c : c + 1, :] = gain_sum_s[:, 128 * c : 128 * c + 128]
        gain_send[0, 4 + c : 5 + c, :] = gain_sum_t[:, 128 * c : 128 * c + 128]

    def send_gain_s(i):
        p = lax.rem(station + i, 8)
        remote(gain_send.at[0], gain_s_recv.at[station], R_GAIN_S, (dp, p, tm))

    each(1, 8, send_gain_s)
    gain_s_recv[station] = gain_send[0]

    sums_own(0, ups_s[...])
    sums_first(0, R_STATION)
    sums_third(1, R_TIME)

    received(gain_s_recv.at[pl.ds(0, 7)], R_GAIN_S)
    value = gain_s_recv[0]
    for j in range(1, 8):
        value = value + gain_s_recv[j]
    gain_send[1] = value

    def send_gain_x(i):
        p = lax.rem(x_at + i, 4)
        remote(gain_send.at[1], gain_x_recv.at[x_at], R_GAIN_X, (dp, station, z_hi * 4 + p))

    each(1, 4, send_gain_x)
    gain_x_recv[x_at] = value
    sums_end(1, R_TIME)

    received(gain_x_recv.at[pl.ds(0, 3)], R_GAIN_X)
    value = gain_x_recv[0]
    for j in range(1, 4):
        value = value + gain_x_recv[j]
    gain_send[2] = value
    mine = 2 * z_hi + dp

    def send_gain_z(i):
        p = lax.rem(mine + i, 8)
        remote(
            gain_send.at[2], gain_z_recv.at[mine], R_GAIN_Z,
            (lax.rem(p, 2), station, (p // 2) * 4 + x_at),
        )

    each(1, 8, send_gain_z)
    gain_z_recv[mine] = value

    sums_second(0, R_STATION)

    received(gin_recv.at[pl.ds(0, 7)], R_GIN)
    for s in range(8):
        for e in range(2):
            for st in range(2):
                for c in range(4):
                    fine[c, pl.ds(st * 16 + 2 * s + e, 16, stride=32), :] = gin_recv[
                        s, e, st, :, 128 * c : 128 * c + 128
                    ].astype(F32)
    for c in range(4):
        x_raw[:, :, 128 * c : 128 * c + 128] = fine[c].astype(BF).reshape(32, 16, 128)
    result = local_copy(x_raw, gin_hbm, L_OUT)
    result.start()

    sums_third(0, R_STATION)
    received(gain_z_recv.at[pl.ds(0, 7)], R_GAIN_Z)
    value = gain_z_recv[0]
    for j in range(1, 8):
        value = value + gain_z_recv[j]
    gains_ref[...] = value

    for e in range(2):
        sent(in_send.at[pl.ds(0, 7), e], R_INS[e])
    for st in range(2):
        sent(cot_recv.at[st, pl.ds(0, 15)], R_COTS[st])
    for part in range(2):
        sent(mid_send.at[part, pl.ds(0, 63 + part)], R_MID + part)
        sent(gmid_send.at[part, pl.ds(0, 63 + part)], R_GMID + part)
    sent(gin_recv.at[pl.ds(0, 7)], R_GIN)
    sent(gain_s_recv.at[pl.ds(0, 7)], R_GAIN_S)
    sent(gain_x_recv.at[pl.ds(0, 3)], R_GAIN_X)
    sent(gain_z_recv.at[pl.ds(0, 7)], R_GAIN_Z)
    for layer, base in ((1, R_TIME), (0, R_STATION)):
        sent(pair_send.at[layer], base + PAIR)
        sent(y_recv.at[layer, pl.ds(0, 3)], base + FIRST_Y)
        sent(x1_recv.at[layer, pl.ds(0, 3)], base + FIRST_X)
        sent(xb_recv.at[layer, pl.ds(0, 3)], base + SECOND_X)
        sent(yb_recv.at[layer, pl.ds(0, 3)], base + SECOND_Y)
        sent(z_recv.at[layer, pl.ds(0, 7)], base + THIRD)
    sums_end(0, R_STATION)
    result.wait()


def deliver(gin, sums, gains, gin_ref, gq_s_ref, go_s_ref, gg_s_ref, gq_t_ref, go_t_ref, gg_t_ref):
    gin_ref[...] = gin[...]
    for layer, qkv_ref, out_ref in ((0, gq_s_ref, go_s_ref), (1, gq_t_ref, go_t_ref)):
        value = sums[layer].astype(F32)
        qkv_ref[...] = value[:, 0:96].astype(BF)
        out_ref[...] = value.T[96:128].astype(BF)
    for c in range(4):
        gg_s_ref[:, 128 * c : 128 * c + 128] = gains[c : c + 1]
        gg_t_ref[:, 128 * c : 128 * c + 128] = gains[4 + c : 5 + c]


def local(inputs, cotangent, station_gain, station_qkv, station_out, time_gain, time_qkv, time_out):
    any_space = pl.BlockSpec(memory_space=pl.ANY)
    vmem = pl.BlockSpec(memory_space=pltpu.VMEM)
    shape = jax.ShapeDtypeStruct
    merged = pl.pallas_call(
        kernel,
        out_shape=(shape((32, 16, WIDTH), BF), shape((2, 64, 128), BF), shape((8, 128), F32)),
        in_specs=[any_space, any_space, vmem, any_space, any_space, vmem, any_space, any_space],
        out_specs=[any_space, vmem, vmem],
        scratch_shapes=[
            pltpu.VMEM((32, 16, WIDTH), BF),
            pltpu.VMEM((4, TOKENS, 128), F32),
            pltpu.VMEM((PEERS * 16, 128), F32),
            pltpu.VMEM((8, 2, 2, 16, WIDTH), BF),
            pltpu.VMEM((2, 2, 2, 4, 16, WIDTH), BF),
            pltpu.VMEM((2, 16, 16, WIDTH), BF),
            pltpu.VMEM((2, 2, 2, 4, 16, WIDTH), BF),
            pltpu.VMEM((WIDTH, 3 * WIDTH), BF),
            pltpu.VMEM((WIDTH, WIDTH), BF),
            pltpu.VMEM((WIDTH, 3 * WIDTH), BF),
            pltpu.VMEM((WIDTH, WIDTH), BF),
            pltpu.VMEM((2, TOKENS, WIDTH), BF),
            pltpu.VMEM((TOKENS, 3 * WIDTH), BF),
            pltpu.VMEM((TOKENS, 3 * WIDTH), BF),
            pltpu.VMEM((8, SEQ, 2 * SEQ), F32),
            pltpu.VMEM((2, TOKENS, WIDTH), BF),
            pltpu.VMEM((TOKENS, WIDTH), BF),
            pltpu.VMEM((TOKENS, 3 * WIDTH), BF),
            pltpu.VMEM((2, 4, 2, 64, TOKENS), BF),
            pltpu.VMEM((2, 4, 2, 64, TOKENS), BF),
            pltpu.VMEM((2, 64, 16, 128), BF),
            pltpu.VMEM((2, 64, 16, 128), BF),
            pltpu.VMEM((TOKENS, WIDTH), F32),
            pltpu.VMEM((2, 64, 16, 128), BF),
            pltpu.VMEM((2, 64, 16, 128), BF),
            pltpu.VMEM((TOKENS, WIDTH), BF),
            pltpu.VMEM((2, 2, 2, 4, 16, WIDTH), BF),
            pltpu.VMEM((8, 2, 2, 16, WIDTH), BF),
            pltpu.VMEM((4, 64, 4 * WIDTH), F32),
            pltpu.VMEM((2, 4, 64, 4 * WIDTH), BF),
            pltpu.VMEM((2, 4, 64, 4 * WIDTH), BF),
            pltpu.VMEM((2, 4, 16, 32, 128), BF),
            pltpu.VMEM((2, 4, 16, 32, 128), BF),
            pltpu.VMEM((2, 4, 4, 4, 32, 128), BF),
            pltpu.VMEM((2, 4, 4, 4, 32, 128), BF),
            pltpu.VMEM((2, 4, 4, 32, 128), BF),
            pltpu.VMEM((2, 4, 4, 32, 128), BF),
            pltpu.VMEM((2, 4, 4, 32, 128), BF),
            pltpu.VMEM((2, 4, 4, 32, 128), BF),
            pltpu.VMEM((2, 4, 64, 128), BF),
            pltpu.VMEM((2, 8, 64, 128), BF),
            pltpu.VMEM((3, 8, 128), F32),
            pltpu.VMEM((8, 8, 128), F32),
            pltpu.VMEM((4, 8, 128), F32),
            pltpu.VMEM((8, 8, 128), F32),
            pltpu.SemaphoreType.DMA((N_SEMS,)),
            pltpu.SemaphoreType.DMA((N_SEMS,)),
            pltpu.SemaphoreType.DMA((7,)),
        ],
        compiler_params=pltpu.CompilerParams(
            collective_id=0, has_side_effects=True, vmem_limit_bytes=60 * 2**20
        ),
    )(
        inputs.reshape(32, 16, WIDTH), cotangent.reshape(32, 16, WIDTH),
        station_gain.reshape(1, WIDTH), station_qkv, station_out,
        time_gain.reshape(1, WIDTH), time_qkv, time_out,
    )
    grad_in, qkv_s, out_s, gain_s, qkv_t, out_t, gain_t = pl.pallas_call(
        deliver,
        out_shape=(
            shape((32, 16, WIDTH), BF),
            shape((64, 96), BF), shape((32, 64), BF), shape((1, WIDTH), F32),
            shape((64, 96), BF), shape((32, 64), BF), shape((1, WIDTH), F32),
        ),
        in_specs=[vmem] * 3,
        out_specs=[vmem] * 7,
    )(*merged)
    return (
        grad_in.reshape(inputs.shape),
        qkv_s, out_s.T, gain_s.reshape(WIDTH), qkv_t, out_t.T, gain_t.reshape(WIDTH),
    )


def solution(mesh):
    rows = P("dp", "station", "tm", None)
    split = P("station", "tm")
    return jax.shard_map(
        local,
        mesh=mesh,
        in_specs=(rows, rows, P(), P(), P(), P(), P(), P()),
        out_specs=(rows, split, split, P(), split, split, P()),
        check_vma=False,
    )
```
